128 devices in a mesh: enc: 2 (over core), img: 64 (over y, z, x).
Axes of the slice: x: 4, y: 4, z: 4, core: 2. Of those that a mesh axis runs over, the one named last changes fastest.
Arguments:
- real_images: bfloat16 [4096, 3072], P('img'), may hold values from -6 to 6
- real_labels: int32 [4096], P('img'), may hold values from 0 to 21840, as said below
- class_ids: int32 [64], replicated, may hold values from 0 to 21840, as said below
- synthetic: float32 [640, 3072], P('img'), may hold values from -6 to 6
- patch_weight: bfloat16 [4, 192, 768], P('enc', 'img'), may hold values from -0.4375 to 0.4375
- position: bfloat16 [4, 16, 768], P('enc'), may hold values from -3 to 3
- qkv_weight: bfloat16 [4, 768, 2304], P('enc', 'img'), may hold values from -0.21875 to 0.21875
- out_weight: bfloat16 [4, 768, 768], P('enc', 'img'), may hold values from -0.21875 to 0.21875
Outputs:
- real_means: float32 [4, 64, 768], P('enc', 'img')
- pixel_grad: float32 [640, 3072], P('img')
The draws below stay inside these ranges and needn't reach their ends.
Inputs may be any that keep to these rules, and one draw needn't show every extreme that they name: class_ids are distinct. `real_labels`: every label is one of class_ids; classes are unevenly represented.
All inputs are finite; a program needn't handle non-finite values.
Results may differ from the reference program's by a relative error of at most 0.014.
Values may be sent and summed in bfloat16 or wider, within the bound.
No kernel may reach another device: no remote copies, remote signals or barrier semaphores. Data moves between devices by JAX's collectives and lax.ppermute only.
A program may use at most 192 MiB of HBM per device.

```python
import jax
import jax.numpy as jnp
from jax import lax

D = 768
HEADS = 12
HEAD_DIM = 64
PATCHES = 16
PATCH_DIM = 192
PIXELS = 3072
IPC = 10
SAMPLED = 64
ENCODERS = 4
NREAL = 4096
CLASSES = 21841


def pick_classes(key):
    first, second = jax.random.split(key)
    inner = jax.random.permutation(first, CLASSES - 2)[:SAMPLED - 2].astype(jnp.int32) + 1
    ends = jnp.array([CLASSES - 1, 0], jnp.int32)
    base = jnp.concatenate([ends, inner])
    order = jax.random.permutation(second, SAMPLED)
    return jnp.take(base, order).astype(jnp.int32)


def draw_class_ids(key, part):
    chosen = pick_classes(key)
    return chosen


def draw_real_labels(key, part):
    chosen = pick_classes(key)
    key = jax.random.fold_in(key, 7)
    first, second, third = jax.random.split(key, 3)
    index = jax.random.randint(first, (NREAL,), 0, SAMPLED)
    index = jnp.minimum(index, jax.random.randint(second, (NREAL,), 0, SAMPLED))
    index = jnp.minimum(index, jax.random.randint(third, (NREAL,), 0, SAMPLED))
    labels = jnp.take(chosen, index).astype(jnp.int32)
    labels = labels.at[0].set(CLASSES - 1)
    labels = labels.at[1].set(0)
    return labels.astype(jnp.int32)


def steps_of(own_key, dims, pieces, least, largest):
    level, own = 1.0, jax.random.fold_in(own_key, 6)
    for axis_at, parts in pieces:
        steps = jnp.exp(jax.random.uniform(jax.random.fold_in(own, axis_at), (parts,), jnp.float32, least / len(pieces), largest / len(pieces)))
        level = level * jnp.repeat(steps, dims[axis_at] // parts).reshape([-1 if axis == axis_at else 1 for axis in range(len(dims))])
    return level


def bell_draw(own_key, dims, spread, limit, cuts=(), dtype=jnp.bfloat16):
    values = spread * jax.random.normal(own_key, dims, jnp.float32)
    if cuts:
        values = values * steps_of(own_key, dims, cuts, -0.22, 0.18)
    return jnp.clip(values, -limit, limit).astype(dtype)


def setup_inputs(seed: int = 0) -> dict:
    streams_of = jax.random.split(jax.random.key(seed), 9)
    real_images = bell_draw(streams_of[0], (NREAL, PIXELS), 1.0, 6.0, ((0, 64),))
    real_labels = draw_real_labels(jax.random.fold_in(streams_of[8], 71), 0)
    class_ids = draw_class_ids(jax.random.fold_in(streams_of[8], 71), 0)
    synthetic = bell_draw(streams_of[3], (SAMPLED * IPC, PIXELS), 1.0, 6.0, ((0, 64),), jnp.float32)
    patch_weight = bell_draw(streams_of[4], (ENCODERS, PATCH_DIM, D), PATCH_DIM ** -0.5, 0.4375, ((0, 2), (1, 64)))
    position = bell_draw(streams_of[5], (ENCODERS, PATCHES, D), 0.5, 3.0, ((0, 2),))
    qkv_weight = bell_draw(streams_of[6], (ENCODERS, D, 3 * D), D ** -0.5, 0.21875, ((0, 2), (1, 64)))
    out_weight = bell_draw(streams_of[7], (ENCODERS, D, D), D ** -0.5, 0.21875, ((0, 2), (1, 64)))
    return {"real_images": real_images, "real_labels": real_labels, "class_ids": class_ids, "synthetic": synthetic, "patch_weight": patch_weight, "position": position, "qkv_weight": qkv_weight, "out_weight": out_weight}


def layer_norm(h):
    mean = lax.optimization_barrier(jnp.mean(h, axis=-1, keepdims=True))
    centred = h - mean
    var = lax.optimization_barrier(jnp.mean(centred * centred, axis=-1, keepdims=True))
    return centred / jnp.sqrt(var + 1e-06)

def encode(pixels, patch_w, pos, qkv_w, out_w):
    count = pixels.shape[0]
    patches = pixels.astype(jnp.bfloat16).reshape(count * PATCHES, PATCH_DIM)
    embed = jnp.dot(patches, patch_w, preferred_element_type=jnp.float32).reshape(count, PATCHES, D)
    embed = embed + pos.astype(jnp.float32)
    normed = layer_norm(embed).astype(jnp.bfloat16).reshape(count * PATCHES, D)
    qkv = jnp.dot(normed, qkv_w, preferred_element_type=jnp.float32).astype(jnp.bfloat16)
    qkv = qkv.reshape(count, PATCHES, 3, HEADS, HEAD_DIM).astype(jnp.float32)
    query, keys, values = (qkv[:, :, 0], qkv[:, :, 1], qkv[:, :, 2])
    scores = jnp.einsum('nqhd,nkhd->nhqk', query, keys) * HEAD_DIM ** (-0.5)
    probs = jax.nn.softmax(scores, axis=-1).astype(jnp.bfloat16).astype(jnp.float32)
    attended = jnp.einsum('nhqk,nkhd->nqhd', probs, values).astype(jnp.bfloat16)
    attended = attended.reshape(count * PATCHES, D)
    hidden = embed + jnp.dot(attended, out_w, preferred_element_type=jnp.float32).reshape(count, PATCHES, D)
    return lax.optimization_barrier(jnp.mean(layer_norm(hidden), axis=1))

def reference(real_images, real_labels, class_ids, synthetic, patch_weight, position, qkv_weight, out_weight):
    onehot = (real_labels[None, :] == class_ids[:, None]).astype(jnp.bfloat16)
    counts = lax.optimization_barrier(jnp.sum(onehot.astype(jnp.float32), axis=1))
    means = []
    for enc in range(ENCODERS):
        feats = encode(real_images, patch_weight[enc], position[enc], qkv_weight[enc], out_weight[enc]).astype(jnp.bfloat16)
        sums = jnp.dot(onehot, feats, preferred_element_type=jnp.float32)
        means.append(sums / jnp.maximum(counts, 1.0)[:, None])
    real_means = jnp.stack(means)

    def matching(pixels):
        total = jnp.zeros((), jnp.float32)
        for enc in range(ENCODERS):
            feats = encode(pixels, patch_weight[enc], position[enc], qkv_weight[enc], out_weight[enc])
            synth_mean = lax.optimization_barrier(jnp.mean(feats.reshape(SAMPLED, IPC, D), axis=1))
            diff = synth_mean - real_means[enc]
            total = total + jnp.sum(diff * diff)
        return total
    pixel_grad = jax.grad(matching)(synthetic)
    return (real_means, pixel_grad)
```

```python
import jax
import jax.numpy as jnp
from jax import lax
from jax.experimental import pallas as pl
from jax.experimental.pallas import tpu as pltpu
from jax.sharding import PartitionSpec as P

AXES = ("enc", "img")
BF = jnp.bfloat16
F32 = jnp.float32
D = 768
PIXELS = 3072
IPC = 10
SLOT = 6
SYN = 4 * SLOT
BLOCK_ROWS = 48
COLS = 2 * D + 128
STEP = 16
REAL = 128
TOKENS = 16
VMEM_LIMIT = 56 * 1024 * 1024


def flat(c, y, z, x):
    return (c % 2) * 64 + (y % 4) * 16 + (z % 4) * 4 + (x % 4)


PLACES = [(c, y, z, x) for c in range(2) for y in range(4) for z in range(4) for x in range(4)]


def permute(a, target):
    return lax.ppermute(a, AXES, [(flat(*p), flat(*target(*p))) for p in PLACES])


def swap_cores(a):
    return permute(a, lambda c, y, z, x: (1 - c, y, z, x))


def from_x(a, k):
    return permute(a, lambda c, y, z, x: (c, y, z, x - k))


def from_first(a, k):
    return permute(a, lambda c, y, z, x: (c, y - k, z, x) if c == 0 else (c, y, z - k, x))


def from_second(a, k):
    return permute(a, lambda c, y, z, x: (c, y, z - k, x) if c == 0 else (c, y - k, z, x))


def normalise(h):
    mean = jnp.mean(h, axis=-1, keepdims=True)
    centred = h - mean
    var = jnp.mean(centred * centred, axis=-1, keepdims=True)
    rstd = lax.rsqrt(var + 1e-06)
    return centred * rstd, rstd


def dot(a, b):
    return jnp.dot(a, b, preferred_element_type=F32)


def dot_nt(a, b):
    return lax.dot_general(a, b, (((1,), (1,)), ((), ())), preferred_element_type=F32)


def dot_tn(a, b):
    return lax.dot_general(a, b, (((0,), (0,)), ((), ())), preferred_element_type=F32)


def low_half():
    return lax.broadcasted_iota(jnp.int32, (128, 128), 1) < 64


def by_head(a, low):
    zero = jnp.zeros_like(a)
    return jnp.concatenate([jnp.where(low, a, zero), jnp.where(low, zero, a)], axis=0)


def image_bias():
    row = lax.broadcasted_iota(jnp.int32, (128, 128), 0)
    col = lax.broadcasted_iota(jnp.int32, (128, 128), 1)
    return jnp.where(row % 8 == col % 8, 0.0, -1e30).astype(F32)


def embed_tiles(x32, wp_ref, posx, tiles):
    halves = []
    for odd in range(2):
        rows = [
            x32[8 * t : 8 * t + 8, 384 * j + 128 * odd : 384 * j + 128 * odd + 256]
            for t in range(tiles)
            for j in range(8)
        ]
        halves.append(dot(jnp.concatenate(rows, axis=0).astype(BF), wp_ref[odd]))
    return [
        jnp.concatenate([h[64 * t : 64 * t + 64] for h in halves], axis=0) + posx
        for t in range(tiles)
    ]


def scores_exp(q, kbd, bias):
    s = dot_nt(q, kbd)
    parts = []
    for h in range(2):
        sh = s[:, 128 * h : 128 * h + 128] + bias
        parts.append(jnp.exp(sh - jnp.max(sh, axis=-1, keepdims=True)))
    return jnp.concatenate(parts, axis=1)


def real_kernel(
    where_ref, x_ref, posx_ref, l0, l1, l2, l3, o0, o1, o2, o3,
    csum_ref, w_ref, wp_ref, e_ref, n_ref, qkv_ref, att_ref, feat_ref, hot_ref, sems,
):
    step = pl.program_id(0)
    tiles = STEP // 8

    @pl.when(step == 0)
    def _():
        core, y, z = where_ref[0], where_ref[1], where_ref[2]
        copies = []
        for other, refs in enumerate(((l0, l1, l2, l3), (o0, o1, o2, o3))):
            part = lax.rem(core + other, 2)
            for j in range(4):
                for i in range(4):
                    dy = jnp.where(part == 0, i, j)
                    dz = jnp.where(part == 0, j, i)
                    block = lax.rem(y + dy, 4) * 4 + lax.rem(z + dz, 4)
                    row = pl.multiple_of(block * BLOCK_ROWS, 16)
                    copies.append(
                        pltpu.make_async_copy(
                            refs[j].at[i],
                            w_ref.at[part, pl.ds(row, BLOCK_ROWS), :],
                            sems.at[other * 16 + j * 4 + i],
                        )
                    )
        for copy in copies:
            copy.start()
        for copy in copies:
            copy.wait()
        out_row = lax.broadcasted_iota(jnp.int32, (192, D), 0)
        in_row = lax.broadcasted_iota(jnp.int32, (192, D), 1)
        wp_ref[...] = jnp.zeros_like(wp_ref)
        for j in range(3):
            pick = jnp.where(in_row == 4 * out_row + j, 1.0, 0.0).astype(BF)
            for part in range(2):
                piece = dot(pick, w_ref[part, :, 2 * D :]).astype(BF)
                at = 384 * part + 128 * j
                wp_ref[0, 0:192, at : at + 128] = piece
                wp_ref[1, 64:256, at : at + 128] = piece

    x32 = x_ref[...].astype(F32)
    for t, e in enumerate(embed_tiles(x32, wp_ref, posx_ref[...], tiles)):
        e_ref[128 * t : 128 * t + 128] = e
        n_ref[128 * t : 128 * t + 128] = normalise(e)[0].astype(BF)
    normed = n_ref[...]
    qkv_ref[:, : 2 * D] = dot(normed, w_ref[0, :, : 2 * D]).astype(BF)
    qkv_ref[:, 2 * D :] = dot(normed, w_ref[1, :, :D]).astype(BF)
    low = low_half()
    bias = image_bias()
    ones = by_head(jnp.ones((128, 128), BF), low)
    for t in range(tiles):
        rows = slice(128 * t, 128 * t + 128)
        for p in range(6):
            at = 128 * p
            q = qkv_ref[rows, at : at + 128] * jnp.asarray(0.125, BF)
            kbd = by_head(qkv_ref[rows, D + at : D + at + 128], low)
            vbd = by_head(qkv_ref[rows, 2 * D + at : 2 * D + at + 128], low)
            ex = scores_exp(q, kbd, bias).astype(BF)
            o = dot(ex, jnp.concatenate([vbd, ones], axis=1))
            att_ref[rows, at : at + 128] = (o[:, :128] / o[:, 128:]).astype(BF)
    hidden = e_ref[...] + dot(att_ref[...], w_ref[1, :, D : 2 * D])
    feats = []
    for t in range(tiles):
        xhat = normalise(hidden[128 * t : 128 * t + 128])[0]
        feats.append(jnp.sum(xhat.reshape(TOKENS, 8, D), axis=0) * (1.0 / TOKENS))
    at = pl.multiple_of(step * STEP, STEP)
    feat_ref[pl.ds(at, STEP), :D] = jnp.concatenate(feats, axis=0).astype(BF)
    feat_ref[pl.ds(at, STEP), D:] = jnp.ones((STEP, 128), BF)
    cls = lax.broadcasted_iota(jnp.int32, (STEP, 128), 1).astype(F32)
    hot_ref[pl.ds(at, STEP), :] = jnp.where(x32[:, PIXELS:] == cls, 1.0, 0.0).astype(BF)

    @pl.when(step == REAL // STEP - 1)
    def _():
        csum_ref[...] = dot_tn(hot_ref[...], feat_ref[...])[:64].astype(csum_ref.dtype)


def synth_kernel(
    x_ref, posx_ref, w_ref, wp_ref,
    feat_ref, xhat1_ref, r1_ref, qkv_ref, p_ref, xhat2_ref, r2_ref, e_ref, n_ref, att_ref,
):
    tiles = SYN // 8
    x32 = x_ref[...].astype(F32)
    for t, e in enumerate(embed_tiles(x32, wp_ref, posx_ref[...], tiles)):
        rows = slice(128 * t, 128 * t + 128)
        e_ref[rows] = e
        xhat, rstd = normalise(e)
        xhat1_ref[rows] = xhat
        r1_ref[rows] = jnp.broadcast_to(rstd, (128, 128))
        n_ref[rows] = xhat.astype(BF)
    normed = n_ref[...]
    qkv_ref[:, : 2 * D] = dot(normed, w_ref[0, :, : 2 * D]).astype(BF)
    qkv_ref[:, 2 * D :] = dot(normed, w_ref[1, :, :D]).astype(BF)
    low = low_half()
    bias = image_bias()
    for t in range(tiles):
        rows = slice(128 * t, 128 * t + 128)
        for p in range(6):
            at = 128 * p
            q = qkv_ref[rows, at : at + 128] * jnp.asarray(0.125, BF)
            kbd = by_head(qkv_ref[rows, D + at : D + at + 128], low)
            vbd = by_head(qkv_ref[rows, 2 * D + at : 2 * D + at + 128], low)
            ex = scores_exp(q, kbd, bias)
            probs = jnp.concatenate(
                [
                    ex[:, 128 * h : 128 * h + 128]
                    / jnp.sum(ex[:, 128 * h : 128 * h + 128], axis=-1, keepdims=True)
                    for h in range(2)
                ],
                axis=1,
            ).astype(BF)
            p_ref[rows, 256 * p : 256 * p + 256] = probs
            att_ref[rows, at : at + 128] = dot(probs, vbd).astype(BF)
    hidden = e_ref[...] + dot(att_ref[...], w_ref[1, :, D : 2 * D])
    for t in range(tiles):
        rows = slice(128 * t, 128 * t + 128)
        xhat, rstd = normalise(hidden[rows])
        xhat2_ref[rows] = xhat
        r2_ref[rows] = jnp.broadcast_to(rstd, (128, 128))
        feat_ref[8 * t : 8 * t + 8] = jnp.sum(xhat.reshape(TOKENS, 8, D), axis=0) * (1.0 / TOKENS)


def norm_back(g, xhat, rstd):
    mean_g = jnp.mean(g, axis=-1, keepdims=True)
    mean_gx = jnp.mean(g * xhat, axis=-1, keepdims=True)
    return rstd[:, :1] * (g - mean_g - xhat * mean_gx)


def back_kernel(
    g_ref, w_ref, wp_ref, xhat1_ref, r1_ref, qkv_ref, p_ref, xhat2_ref, r2_ref,
    out_ref, dh_ref, dhb_ref, da_ref, dqkv_ref,
):
    tiles = SYN // 8
    for t in range(tiles):
        rows = slice(128 * t, 128 * t + 128)
        g = jnp.broadcast_to(g_ref[8 * t : 8 * t + 8][None], (TOKENS, 8, D)).reshape(128, D)
        dh = norm_back(g, xhat2_ref[rows], r2_ref[rows])
        dh_ref[rows] = dh
        dhb_ref[rows] = dh.astype(BF)
    da_ref[...] = dot_nt(dhb_ref[...], w_ref[1, :, D : 2 * D]).astype(BF)
    low = low_half()
    for t in range(tiles):
        rows = slice(128 * t, 128 * t + 128)
        for p in range(6):
            at = 128 * p
            q = qkv_ref[rows, at : at + 128]
            kbd = by_head(qkv_ref[rows, D + at : D + at + 128], low)
            vbd = by_head(qkv_ref[rows, 2 * D + at : 2 * D + at + 128], low)
            da = da_ref[rows, at : at + 128]
            probs = p_ref[rows, 256 * p : 256 * p + 256]
            p32 = probs.astype(F32)
            dp = dot_nt(da, vbd)
            ds = []
            for h in range(2):
                ph, dph = p32[:, 128 * h : 128 * h + 128], dp[:, 128 * h : 128 * h + 128]
                inner = jnp.sum(ph * dph, axis=-1, keepdims=True)
                ds.append(ph * (dph - inner) * 0.125)
            ds = jnp.concatenate(ds, axis=1).astype(BF)
            dqkv_ref[rows, at : at + 128] = dot(ds, kbd).astype(BF)
            dk = dot_tn(ds, q)
            dqkv_ref[rows, D + at : D + at + 128] = jnp.where(low, dk[:128], dk[128:]).astype(BF)
            dv = dot_tn(probs, da)
            dqkv_ref[rows, 2 * D + at : 2 * D + at + 128] = jnp.where(
                low, dv[:128], dv[128:]
            ).astype(BF)
    dn = dot_nt(dqkv_ref[:, : 2 * D], w_ref[0, :, : 2 * D])
    dn = dn + dot_nt(dqkv_ref[:, 2 * D :], w_ref[1, :, :D])
    for t in range(tiles):
        rows = slice(128 * t, 128 * t + 128)
        de = dh_ref[rows] + norm_back(dn[rows], xhat1_ref[rows], r1_ref[rows])
        dhb_ref[rows] = de.astype(BF)
    pieces = []
    for t in range(tiles):
        even = dot_nt(dhb_ref[128 * t : 128 * t + 64], wp_ref[0])
        odd = dot_nt(dhb_ref[128 * t + 64 : 128 * t + 128], wp_ref[1])
        pieces.append(
            jnp.concatenate([even[:, :128], even[:, 128:] + odd[:, :128], odd[:, 128:]], axis=1)
        )
    for j in range(8):
        out_ref[:, 384 * j : 384 * j + 384] = jnp.concatenate(
            [piece[8 * j : 8 * j + 8] for piece in pieces], axis=0
        ).astype(BF)


def full_spec(shape):
    return pl.BlockSpec(shape, lambda *_: (0,) * len(shape))


def run_real(place, x, posx, mine, theirs):
    steps = REAL // STEP
    rows = STEP * TOKENS
    return pl.pallas_call(
        real_kernel,
        grid=(steps,),
        in_specs=[
            pl.BlockSpec(memory_space=pltpu.SMEM),
            pl.BlockSpec((STEP, PIXELS + 128), lambda i: (i, 0)),
            full_spec((128, D)),
        ]
        + [pl.BlockSpec(memory_space=pl.ANY)] * 8,
        out_specs=[full_spec((64, D + 128)), full_spec((2, D, COLS)), full_spec((2, 256, D))],
        out_shape=[
            jax.ShapeDtypeStruct((64, D + 128), BF),
            jax.ShapeDtypeStruct((2, D, COLS), BF),
            jax.ShapeDtypeStruct((2, 256, D), BF),
        ],
        scratch_shapes=[
            pltpu.VMEM((rows, D), F32),
            pltpu.VMEM((rows, D), BF),
            pltpu.VMEM((rows, 3 * D), BF),
            pltpu.VMEM((rows, D), BF),
            pltpu.VMEM((REAL, D + 128), BF),
            pltpu.VMEM((REAL, 128), BF),
            pltpu.SemaphoreType.DMA((32,)),
        ],
        compiler_params=pltpu.CompilerParams(vmem_limit_bytes=VMEM_LIMIT),
        cost_estimate=pl.CostEstimate(
            flops=14_000_000_000, bytes_accessed=12_000_000, transcendentals=3_000_000
        ),
        name="real_forward",
    )(place, x, posx, *mine, *theirs)


def run_synth(x, posx, w, wp):
    rows = SYN * TOKENS
    shapes = [
        ((SYN, D), F32),
        ((rows, D), F32),
        ((rows, 128), F32),
        ((rows, 3 * D), BF),
        ((rows, 2 * D), BF),
        ((rows, D), F32),
        ((rows, 128), F32),
    ]
    return pl.pallas_call(
        synth_kernel,
        out_shape=[jax.ShapeDtypeStruct(s, t) for s, t in shapes],
        scratch_shapes=[
            pltpu.VMEM((rows, D), F32),
            pltpu.VMEM((rows, D), BF),
            pltpu.VMEM((rows, D), BF),
        ],
        compiler_params=pltpu.CompilerParams(vmem_limit_bytes=VMEM_LIMIT),
        cost_estimate=pl.CostEstimate(
            flops=3_000_000_000, bytes_accessed=12_000_000, transcendentals=600_000
        ),
        name="synth_forward",
    )(x, posx, w, wp)


def run_back(g, w, wp, saved):
    rows = SYN * TOKENS
    return pl.pallas_call(
        back_kernel,
        out_shape=jax.ShapeDtypeStruct((SYN, PIXELS), BF),
        scratch_shapes=[
            pltpu.VMEM((rows, D), F32),
            pltpu.VMEM((rows, D), BF),
            pltpu.VMEM((rows, D), BF),
            pltpu.VMEM((rows, 3 * D), BF),
        ],
        compiler_params=pltpu.CompilerParams(vmem_limit_bytes=VMEM_LIMIT),
        cost_estimate=pl.CostEstimate(
            flops=4_000_000_000, bytes_accessed=12_000_000, transcendentals=0
        ),
        name="synth_backward",
    )(g, w, wp, *saved)


def gather_weights(core, x, patch_weight, qkv_weight, out_weight):
    columns = jnp.concatenate([qkv_weight, out_weight], axis=-1)
    patch = jnp.pad(patch_weight.reshape(2, 3, 2, 3, 128), ((0, 0),) * 3 + ((0, 1), (0, 0)))
    patch = patch.transpose(0, 1, 3, 2, 4).reshape(2, 12, 2, 128)
    both = jnp.concatenate([columns.reshape(2, 12, 2, 2 * D), patch], axis=-1)
    both = both.transpose(0, 2, 1, 3).reshape(4, 12, COLS)
    parts = []
    for k in range(4):
        to = (x - k) % 4
        first = to // 2 == core
        index = (to % 2) * 2 + jnp.where(first, 0, 1)

        def target(c, yy, zz, xx, k=k):
            to = (xx - k) % 4
            return (0, yy, zz, to) if to // 2 == c else (1, yy, zz, (to + 2) % 4)

        parts.append(permute(lax.dynamic_index_in_dim(both, index, 0, keepdims=False), target))
    ring = jnp.roll(jnp.stack(parts), x + 2 * core, axis=0).reshape(BLOCK_ROWS, COLS)
    line = jnp.stack([ring] + [from_first(ring, k) for k in (1, 2, 3)])
    mine = [line] + [from_second(line, k) for k in (1, 2, 3)]
    theirs = [swap_cores(a) for a in mine]
    return mine, theirs


def local(
    real_images, real_labels, class_ids, synthetic, patch_weight, position, qkv_weight, out_weight
):
    core, img = lax.axis_index("enc"), lax.axis_index("img")
    y, z, x = img // 16, (img // 4) % 4, img % 4
    place = jnp.stack([core, y, z, x]).astype(jnp.int32)

    hit = real_labels[:, None] == class_ids[None, :]
    index = jnp.sum(jnp.where(hit, jnp.arange(64, dtype=F32)[None, :], 0.0), axis=1)
    tagged = jnp.concatenate(
        [real_images, jnp.broadcast_to(index[:, None], (64, 128)).astype(BF)], axis=1
    )
    syn = lax.dynamic_slice_in_dim(synthetic, 5 * core, 5, 0).astype(BF)
    images = jnp.concatenate(
        [lax.dynamic_slice_in_dim(tagged, 32 * core, 32, 0), jnp.pad(syn, ((0, 1), (0, 128)))],
        axis=0,
    )
    images = jnp.stack([images] + [from_x(images, k) for k in (1, 2, 3)])
    real_x = images[:, :32].reshape(REAL, PIXELS + 128)
    syn_x = images[:, 32:, :PIXELS].reshape(SYN, PIXELS)

    their_pos = swap_cores(position)
    pos = lax.dynamic_index_in_dim(
        jnp.where(x // 2 == core, position, their_pos), x % 2, 0, keepdims=False
    ).astype(F32)
    posx = jnp.repeat(pos.reshape(8, 2, D).transpose(1, 0, 2).reshape(TOKENS, D), 8, axis=0)

    mine, theirs = gather_weights(core, x, patch_weight, qkv_weight, out_weight)
    csum, w, wp = run_real(place, real_x, posx, mine, theirs)

    groups = [[yz * 4 + xx for yz in range(16)] for xx in range(4)]
    got = lax.all_to_all(
        csum.reshape(16, 4, D + 128), "img", 0, 0, axis_index_groups=groups
    )
    half = jnp.sum(got.astype(F32), axis=0)
    total = half + swap_cores(half)
    means = total[:, :D] / jnp.maximum(total[:, D : D + 1], 1.0)

    feats, *saved = run_synth(syn_x, posx, w, wp)
    own = jnp.sum(feats.reshape(4, SLOT, D)[:, :5], axis=1)
    syn_mean = (own + swap_cores(own)) * (1.0 / IPC)
    g = (syn_mean - jnp.roll(means, -x, axis=0)) * (2.0 / (IPC * TOKENS))
    grads = run_back(jnp.repeat(g, SLOT, axis=0), w, wp, saved)

    sent = []
    for m in range(2):
        row = lax.dynamic_index_in_dim(means, (x - m) % 2 + 2 * core, 0, keepdims=True)
        sent.append(
            permute(row, lambda c, yy, zz, xx, m=m: (xx // 2, yy, zz, (xx - m) % 2 + 2 * c))
        )
    first = jnp.where(x % 2 == 0, sent[0], sent[1])
    second = jnp.where(x % 2 == 0, sent[1], sent[0])
    real_means = jnp.stack([first, second])

    grads = grads.reshape(4, SLOT, PIXELS)
    pixel = grads[0].astype(F32)
    for k in (1, 2, 3):
        pixel = pixel + from_x(grads[k], -k).astype(F32)
    pixel = pixel[:5]
    other = swap_cores(pixel)
    pixel_grad = jnp.concatenate(
        [jnp.where(core == 0, pixel, other), jnp.where(core == 0, other, pixel)], axis=0
    )
    return (real_means, pixel_grad)


def solution(mesh):
    return jax.shard_map(
        local,
        mesh=mesh,
        in_specs=(
            P("img", None),
            P("img"),
            P(),
            P("img", None),
            P("enc", "img", None),
            P("enc", None, None),
            P("enc", "img", None),
            P("enc", "img", None),
        ),
        out_specs=(P("enc", "img", None), P("img", None)),
        check_vma=False,
    )
```

```python
import jax
import jax.numpy as jnp
from jax import lax
from jax.experimental import pallas as pl
from jax.experimental.pallas import tpu as pltpu
from jax.sharding import PartitionSpec as P

AXES = ("enc", "img")
BF = jnp.bfloat16
F32 = jnp.float32
D = 768
PIXELS = 3072
IPC = 10
SLOT = 6
SYN = 4 * SLOT
BLOCK_ROWS = 48
COLS = 2 * D + 128
OUT_AT = COLS + D
STEP = 64
QKV_UNROLL = 9
SYN_QKV_UNROLL = 9
REAL = 128
TOKENS = 16
VMEM_LIMIT = 60 * 1024 * 1024


def flat(c, y, z, x):
    return (c % 2) * 64 + (y % 4) * 16 + (z % 4) * 4 + (x % 4)


PLACES = [(c, y, z, x) for c in range(2) for y in range(4) for z in range(4) for x in range(4)]


def permute(a, target):
    return lax.ppermute(a, AXES, [(flat(*p), flat(*target(*p))) for p in PLACES])


def swap_cores(a):
    return permute(a, lambda c, y, z, x: (1 - c, y, z, x))


def from_x(a, k):
    return permute(a, lambda c, y, z, x: (c, y, z, x - k))


def from_first(a, k):
    return permute(a, lambda c, y, z, x: (c, y - k, z, x) if c == 0 else (c, y, z - k, x))


def from_second(a, k):
    return permute(a, lambda c, y, z, x: (c, y, z - k, x) if c == 0 else (c, y - k, z, x))


def normalise(h):
    mean = jnp.mean(h, axis=-1, keepdims=True)
    centred = h - mean
    var = jnp.mean(centred * centred, axis=-1, keepdims=True)
    rstd = lax.rsqrt(var + 1e-06)
    return centred * rstd, rstd


def dot(a, b):
    return jnp.dot(a, b, preferred_element_type=F32)


def dot_nt(a, b):
    return lax.dot_general(a, b, (((1,), (1,)), ((), ())), preferred_element_type=F32)


def dot_tn(a, b):
    return lax.dot_general(a, b, (((0,), (0,)), ((), ())), preferred_element_type=F32)


def low_half():
    return lax.broadcasted_iota(jnp.int32, (128, 128), 1) < 64


def by_head(a, low):
    zero = jnp.zeros_like(a)
    return jnp.concatenate([jnp.where(low, a, zero), jnp.where(low, zero, a)], axis=0)


def image_bias():
    row = lax.broadcasted_iota(jnp.int32, (128, 128), 0)
    col = lax.broadcasted_iota(jnp.int32, (128, 128), 1)
    return jnp.where(row % 8 == col % 8, 0.0, -1e30).astype(F32)


def embed_rows(x32, wp_ref, tiles):
    halves = []
    for odd in range(2):
        rows = [
            x32[8 * t : 8 * t + 8, 384 * j + 128 * odd : 384 * j + 128 * odd + 256]
            for t in range(tiles)
            for j in range(8)
        ]
        halves.append(dot(jnp.concatenate(rows, axis=0).astype(BF), wp_ref[odd]))
    return [
        jnp.concatenate([h[64 * t : 64 * t + 64] for h in halves], axis=0) for t in range(tiles)
    ]


def exp_scores(s, bias):
    parts = []
    for h in range(2):
        sh = s[:, 128 * h : 128 * h + 128] + bias
        parts.append(jnp.exp(sh - jnp.max(sh, axis=-1, keepdims=True)))
    return parts


def pipeline(count, first, second, third):
    made = {}
    for k in range(count + 2):
        if k < count:
            made[k] = first(k)
        if 0 <= k - 2 < count:
            third(k - 2, *made.pop(k - 2))
        if 0 <= k - 1 < count:
            out = second(k - 1, made.pop(k - 1))
            made[k - 1] = () if out is None else (out,)


def loop(count, fn, unroll=1):
    def body(i, carry):
        fn(i)
        return carry

    lax.fori_loop(0, count, body, 0, unroll=unroll)


def mult(value, of):
    return value if isinstance(value, int) else pl.multiple_of(value, of)


def patch_sum(xhat):
    return jnp.sum(xhat.reshape(TOKENS, 8, D), axis=0) * (1.0 / TOKENS)


def qkv_product(n_ref, w_ref, qkv_ref, unroll):
    def chunk(c):
        at = mult(256 * c, 128)
        col = mult(256 * c + jnp.where(c >= 6, 128, 0), 128)
        out = dot(n_ref[...], w_ref[:, pl.ds(col, 256)])
        qkv_ref[:, pl.ds(at, 256)] = (out * jnp.where(c < 3, 0.125, 1.0)).astype(BF)

    loop(9, chunk, unroll)


def out_product(att_ref, w_ref, e_ref):
    def chunk(c):
        at = mult(256 * c, 128)
        e_ref[:, pl.ds(at, 256)] += dot(att_ref[...], w_ref[:, pl.ds(OUT_AT + at, 256)])

    loop(3, chunk, 3)


def spread_position(where_ref, mine_ref, theirs_ref, posx_ref):
    core, x = where_ref[0], where_ref[3]
    local = x // 2 == core
    pos = jnp.where(local, mine_ref[lax.rem(x, 2)], theirs_ref[lax.rem(x, 2)]).astype(F32)
    for patch in range(TOKENS):
        at = (patch % 2) * 64 + (patch // 2) * 8
        posx_ref[at : at + 8] = jnp.broadcast_to(pos[patch : patch + 1], (8, D))


def real_kernel(
    where_ref, mine_ref, theirs_ref, i0, i1, i2, i3,
    l0, l1, l2, l3, l4, l5, l6, l7, o0, o1, o2, o3, o4, o5, o6, o7,
    csum_ref, w_out, wp_out,
    e_ref, n_ref, qkv_ref, att_ref, feat_ref, hot_ref, x_ref, posx_ref, w_ref, wp_ref, sems,
):
    tiles = STEP // 8
    groups = REAL // STEP
    core, y, z = where_ref[0], where_ref[1], where_ref[2]

    for k, ref in enumerate((i0, i1, i2, i3)):
        pltpu.make_async_copy(ref.at[0:32], x_ref.at[32 * k : 32 * k + 32], sems.at[1]).start()
    mine = (l0, l1, l2, l3, l4, l5, l6, l7)
    theirs = (o0, o1, o2, o3, o4, o5, o6, o7)
    for other, refs in enumerate((mine, theirs)):
        part = lax.rem(core + other, 2)
        for j in range(4):
            for i in range(4):
                dy = jnp.where(part == 0, i, j)
                dz = jnp.where(part == 0, j, i)
                block = lax.rem(y + dy, 4) * 4 + lax.rem(z + dz, 4)
                row = pl.multiple_of(block * BLOCK_ROWS, 16)
                pltpu.make_async_copy(
                    refs[2 * j + i // 2].at[i % 2],
                    w_ref.at[pl.ds(row, BLOCK_ROWS), pl.ds(pl.multiple_of(part * COLS, 128), COLS)],
                    sems.at[0],
                ).start()
    wp_ref[...] = jnp.zeros_like(wp_ref)
    spread_position(where_ref, mine_ref, theirs_ref, posx_ref)
    cls = lax.broadcasted_iota(jnp.int32, (REAL, 128), 1).astype(F32)
    pltpu.make_async_copy(x_ref, x_ref, sems.at[1]).wait()
    hot_ref[...] = jnp.where(x_ref[:, PIXELS:].astype(F32) == cls, 1.0, 0.0).astype(BF)
    feat_ref[:, D:] = jnp.ones((REAL, 128), BF)
    pltpu.make_async_copy(w_ref, w_ref, sems.at[0]).wait()
    save_w = pltpu.make_async_copy(w_ref, w_out, sems.at[2])
    save_w.start()
    out_row = lax.broadcasted_iota(jnp.int32, (192, D), 0)
    in_row = lax.broadcasted_iota(jnp.int32, (192, D), 1)

    def decode(j):
        pick = jnp.where(in_row == 4 * out_row + j, 1.0, 0.0).astype(BF)
        for part in range(2):
            piece = dot(pick, w_ref[:, part * COLS + 2 * D : (part + 1) * COLS]).astype(BF)
            at = mult(384 * part + 128 * j, 128)
            wp_ref[0, 0:192, pl.ds(at, 128)] = piece
            wp_ref[1, 64:256, pl.ds(at, 128)] = piece

    loop(3, decode, 3)
    save_wp = pltpu.make_async_copy(wp_ref, wp_out, sems.at[3])
    save_wp.start()
    low = low_half()
    bias = image_bias()
    ones = by_head(jnp.ones((128, 128), BF), low)

    def score(u):
        rows = pl.ds((u // 6) * 128, 128)
        at = (u % 6) * 128
        kbd = by_head(qkv_ref[rows, D + at : D + at + 128], low)
        return dot_nt(qkv_ref[rows, at : at + 128], kbd)

    def soften(u, s):
        return jnp.concatenate(exp_scores(s, bias), axis=1).astype(BF)

    def weigh(u, ex):
        rows = pl.ds((u // 6) * 128, 128)
        at = (u % 6) * 128
        vbd = by_head(qkv_ref[rows, 2 * D + at : 2 * D + at + 128], low)
        o = dot(ex, jnp.concatenate([vbd, ones], axis=1))
        att_ref[rows, at : at + 128] = (o[:, :128] / o[:, 128:]).astype(BF)

    def group(g):
        at = mult(g * STEP, STEP)
        x32 = x_ref[pl.ds(at, STEP), :PIXELS].astype(F32)
        for t, e in enumerate(embed_rows(x32, wp_ref, tiles)):
            e = e + posx_ref[...]
            e_ref[128 * t : 128 * t + 128] = e
            n_ref[128 * t : 128 * t + 128] = normalise(e)[0].astype(BF)
        qkv_product(n_ref, w_ref, qkv_ref, QKV_UNROLL)
        pipeline(6 * tiles, score, soften, weigh)
        out_product(att_ref, w_ref, e_ref)
        feats = [patch_sum(normalise(e_ref[128 * t : 128 * t + 128])[0]) for t in range(tiles)]
        feat_ref[pl.ds(at, STEP), :D] = jnp.concatenate(feats, axis=0).astype(BF)

    loop(groups, group)
    sums = dot_tn(hot_ref[...], feat_ref[...])
    for b in range(16):
        block = sums[4 * b : 4 * b + 4].astype(csum_ref.dtype)
        csum_ref[b] = block
        csum_ref[16 + b] = block
    save_w.wait()
    save_wp.wait()


def copies_of(pairs, sems):
    copies = [pltpu.make_async_copy(src, dst, sems.at[i]) for i, (src, dst) in enumerate(pairs)]
    for copy in copies:
        copy.start()
    return copies


def synth_kernel(
    where_ref, mine_ref, theirs_ref, i0, i1, i2, i3, w_in, wp_in,
    sum_ref, n_out, r1_out, qkv_out, p_out, xhat2_out, r2_out,
    n_ref, r1_ref, qkv_ref, p_ref, xhat2_ref, r2_ref,
    e_ref, att_ref, x_ref, posx_ref, w_ref, wp_ref, in_sems, sems,
):
    tiles = SYN // 8
    pairs = [
        (ref.at[32:48, :PIXELS], x_ref.at[16 * k : 16 * k + 16])
        for k, ref in enumerate((i0, i1, i2, i3))
    ]
    loads = copies_of(pairs + [(wp_in, wp_ref), (w_in, w_ref)], in_sems)
    saves = [
        pltpu.make_async_copy(src, dst, sems.at[i])
        for i, (src, dst) in enumerate(
            (
                (n_ref, n_out), (r1_ref, r1_out), (qkv_ref, qkv_out),
                (p_ref, p_out), (xhat2_ref, xhat2_out), (r2_ref, r2_out),
            )
        )
    ]
    spread_position(where_ref, mine_ref, theirs_ref, posx_ref)
    for copy in loads[:5]:
        copy.wait()
    x32 = jnp.concatenate([x_ref[16 * k : 16 * k + 16].astype(F32)[:SLOT] for k in range(4)], axis=0)
    for t, e in enumerate(embed_rows(x32, wp_ref, tiles)):
        rows = slice(128 * t, 128 * t + 128)
        e = e + posx_ref[...]
        e_ref[rows] = e
        xhat, rstd = normalise(e)
        r1_ref[rows] = jnp.broadcast_to(rstd, (128, 128))
        n_ref[rows] = xhat.astype(BF)
    saves[0].start()
    saves[1].start()
    loads[5].wait()
    qkv_product(n_ref, w_ref, qkv_ref, SYN_QKV_UNROLL)
    saves[2].start()
    low = low_half()
    bias = image_bias()

    def score(u):
        rows, at = pl.ds((u // 6) * 128, 128), (u % 6) * 128
        kbd = by_head(qkv_ref[rows, D + at : D + at + 128], low)
        return dot_nt(qkv_ref[rows, at : at + 128], kbd)

    def soften(u, s):
        rows, at = pl.ds((u // 6) * 128, 128), (u % 6) * 256
        parts = [ex / jnp.sum(ex, axis=-1, keepdims=True) for ex in exp_scores(s, bias)]
        p_ref[rows, at : at + 256] = jnp.concatenate(parts, axis=1).astype(BF)

    def weigh(u):
        rows, at = pl.ds((u // 6) * 128, 128), (u % 6) * 128
        vbd = by_head(qkv_ref[rows, 2 * D + at : 2 * D + at + 128], low)
        att_ref[rows, at : at + 128] = dot(p_ref[rows, 2 * at : 2 * at + 256], vbd).astype(BF)

    pipeline(6 * tiles, score, soften, weigh)
    saves[3].start()
    out_product(att_ref, w_ref, e_ref)
    feats = []
    for t in range(tiles):
        rows = slice(128 * t, 128 * t + 128)
        xhat, rstd = normalise(e_ref[rows])
        xhat2_ref[rows] = xhat.astype(BF)
        r2_ref[rows] = jnp.broadcast_to(rstd, (128, 128))
        feats.append(patch_sum(xhat))
    saves[4].start()
    saves[5].start()
    feats = jnp.concatenate(feats, axis=0)
    for s in range(4):
        sum_ref[s : s + 1] = jnp.sum(feats[SLOT * s : SLOT * s + 5], axis=0, keepdims=True)
    for copy in saves:
        copy.wait()


def norm_back(g, xhat, rstd):
    mean_g = jnp.mean(g, axis=-1, keepdims=True)
    mean_gx = jnp.mean(g * xhat, axis=-1, keepdims=True)
    return rstd[:, :1] * (g - mean_g - xhat * mean_gx)


def back_kernel(
    g_ref, w_in, wp_in, n_in, r1_in, qkv_in, p_in, xhat2_in, r2_in,
    out_ref,
    w_ref, wp_ref, n_ref, r1_ref, qkv_ref, p_ref, xhat2_ref, r2_ref,
    dh_ref, dhb_ref, da_ref, dqkv_ref, dn_ref, spread_ref, px_ref, sems,
):
    tiles = SYN // 8
    out_cols = pl.ds(OUT_AT, D)
    loads = copies_of(
        (
            (xhat2_in, xhat2_ref), (r2_in, r2_ref),
            (w_in.at[:, out_cols], w_ref.at[:, out_cols]),
            (qkv_in, qkv_ref), (p_in, p_ref),
            (w_in.at[:, :OUT_AT], w_ref.at[:, :OUT_AT]),
            (n_in, n_ref), (r1_in, r1_ref), (wp_in, wp_ref),
        ),
        sems,
    )
    image = lax.broadcasted_iota(jnp.int32, (SYN, D), 0)
    spread = jnp.zeros((SYN, D), F32)
    for s in range(4):
        mine = (image >= SLOT * s) & (image < SLOT * s + 5)
        spread = jnp.where(mine, g_ref[s : s + 1], spread)
    spread_ref[...] = spread
    loads[0].wait()
    loads[1].wait()

    def second_norm(t):
        rows = pl.ds(mult(128 * t, 128), 128)
        g = spread_ref[pl.ds(mult(8 * t, 8), 8)]
        g = jnp.broadcast_to(g[None], (TOKENS, 8, D)).reshape(128, D)
        dh = norm_back(g, xhat2_ref[rows].astype(F32), r2_ref[rows])
        dh_ref[rows] = dh
        dhb_ref[rows] = dh.astype(BF)

    loop(tiles, second_norm, tiles)
    loads[2].wait()

    def out_back(c):
        at = mult(256 * c, 128)
        da_ref[:, pl.ds(at, 256)] = dot_nt(
            dhb_ref[...], w_ref[pl.ds(at, 256), OUT_AT : OUT_AT + D]
        ).astype(BF)

    loop(3, out_back, 3)
    loads[3].wait()
    loads[4].wait()
    low = low_half()

    def probs_back(u):
        rows, at = pl.ds((u // 6) * 128, 128), (u % 6) * 128
        da = da_ref[rows, at : at + 128]
        return dot_nt(da, by_head(qkv_ref[rows, 2 * D + at : 2 * D + at + 128], low))

    def scores_back(u, dp):
        rows, at = pl.ds((u // 6) * 128, 128), (u % 6) * 128
        da = da_ref[rows, at : at + 128]
        probs = p_ref[rows, 2 * at : 2 * at + 256]
        dv = dot_tn(probs, da)
        dqkv_ref[rows, 2 * D + at : 2 * D + at + 128] = jnp.where(low, dv[:128], dv[128:]).astype(BF)
        p32 = probs.astype(F32)
        ds = []
        for h in range(2):
            ph, dph = p32[:, 128 * h : 128 * h + 128], dp[:, 128 * h : 128 * h + 128]
            inner = jnp.sum(ph * dph, axis=-1, keepdims=True)
            ds.append(ph * (dph - inner))
        return jnp.concatenate(ds, axis=1).astype(BF)

    def query_key_back(u, ds):
        rows, at = pl.ds((u // 6) * 128, 128), (u % 6) * 128
        kbd = by_head(qkv_ref[rows, D + at : D + at + 128], low)
        dqkv_ref[rows, at : at + 128] = (dot(ds, kbd) * 0.125).astype(BF)
        dk = dot_tn(ds, qkv_ref[rows, at : at + 128])
        dqkv_ref[rows, D + at : D + at + 128] = jnp.where(low, dk[:128], dk[128:]).astype(BF)

    pipeline(6 * tiles, probs_back, scores_back, query_key_back)
    loads[5].wait()

    def qkv_back(c):
        at = mult(256 * c, 128)
        rows = pl.ds(at, 256)
        dn = dot_nt(dqkv_ref[:, : 2 * D], w_ref[rows, : 2 * D])
        dn_ref[:, rows] = dn + dot_nt(dqkv_ref[:, 2 * D :], w_ref[rows, COLS : COLS + D])

    loop(3, qkv_back, 3)
    for copy in loads[6:]:
        copy.wait()

    def first_norm(t):
        rows = pl.ds(mult(128 * t, 128), 128)
        de = dh_ref[rows] + norm_back(dn_ref[rows], n_ref[rows].astype(F32), r1_ref[rows])
        de = de.astype(BF)
        even = dot_nt(de[:64], wp_ref[0])
        odd = dot_nt(de[64:], wp_ref[1])
        px_ref[t] = jnp.concatenate(
            [even[:, :128], even[:, 128:] + odd[:, :128], odd[:, 128:]], axis=1
        )

    loop(tiles, first_norm, tiles)
    for j in range(8):
        out_ref[:, 384 * j : 384 * j + 384] = jnp.concatenate(
            [px_ref[t, 8 * j : 8 * j + 8] for t in range(tiles)], axis=0
        ).astype(BF)


SMEM_SPEC = pl.BlockSpec(memory_space=pltpu.SMEM)
VMEM_SPEC = pl.BlockSpec(memory_space=pltpu.VMEM)
ANY_SPEC = pl.BlockSpec(memory_space=pltpu.HBM)


def buffer(shape, kind):
    return pltpu.VMEM(shape, kind)


def run_real(place, mine_pos, their_pos, images, mine, theirs):
    rows = STEP * TOKENS
    return pl.pallas_call(
        real_kernel,
        in_specs=[SMEM_SPEC, VMEM_SPEC, VMEM_SPEC] + [ANY_SPEC] * 20,
        out_specs=[pl.BlockSpec((32, 4, D + 128), lambda: (0, 0, 0)), ANY_SPEC, ANY_SPEC],
        out_shape=[
            jax.ShapeDtypeStruct((32, 4, D + 128), BF),
            jax.ShapeDtypeStruct((D, 2 * COLS), BF),
            jax.ShapeDtypeStruct((2, 256, D), BF),
        ],
        scratch_shapes=[
            buffer((rows, D), F32),
            buffer((rows, D), BF),
            buffer((rows, 3 * D), BF),
            buffer((rows, D), BF),
            buffer((REAL, D + 128), BF),
            buffer((REAL, 128), BF),
            buffer((REAL, PIXELS + 128), BF),
            buffer((128, D), F32),
            buffer((D, 2 * COLS), BF),
            buffer((2, 256, D), BF),
            pltpu.SemaphoreType.DMA((4,)),
        ],
        compiler_params=pltpu.CompilerParams(vmem_limit_bytes=VMEM_LIMIT),
        cost_estimate=pl.CostEstimate(
            flops=14_000_000_000, bytes_accessed=12_000_000, transcendentals=3_000_000
        ),
        name="real_forward",
    )(place, mine_pos, their_pos, *images, *mine, *theirs)


SYN_ROWS = SYN * TOKENS
SAVED = [
    ((SYN_ROWS, D), BF),
    ((SYN_ROWS, 128), F32),
    ((SYN_ROWS, 3 * D), BF),
    ((SYN_ROWS, 2 * D), BF),
    ((SYN_ROWS, D), BF),
    ((SYN_ROWS, 128), F32),
]
WEIGHTS = [((D, 2 * COLS), BF), ((2, 256, D), BF)]


def run_synth(place, mine_pos, their_pos, images, w, wp):
    return pl.pallas_call(
        synth_kernel,
        in_specs=[SMEM_SPEC, VMEM_SPEC, VMEM_SPEC] + [ANY_SPEC] * 6,
        out_specs=[pl.BlockSpec((4, D), lambda: (0, 0))] + [ANY_SPEC] * 6,
        out_shape=[jax.ShapeDtypeStruct((4, D), F32)]
        + [jax.ShapeDtypeStruct(s, t) for s, t in SAVED],
        scratch_shapes=[buffer(s, t) for s, t in SAVED]
        + [
            buffer((SYN_ROWS, D), F32),
            buffer((SYN_ROWS, D), BF),
            buffer((64, PIXELS), BF),
            buffer((128, D), F32),
        ]
        + [buffer(s, t) for s, t in WEIGHTS]
        + [pltpu.SemaphoreType.DMA((6,)), pltpu.SemaphoreType.DMA((6,))],
        compiler_params=pltpu.CompilerParams(vmem_limit_bytes=VMEM_LIMIT),
        cost_estimate=pl.CostEstimate(
            flops=3_000_000_000, bytes_accessed=12_000_000, transcendentals=600_000
        ),
        name="synth_forward",
    )(place, mine_pos, their_pos, *images, w, wp)


def run_back(g, w, wp, saved):
    return pl.pallas_call(
        back_kernel,
        in_specs=[VMEM_SPEC] + [ANY_SPEC] * 8,
        out_specs=pl.BlockSpec((SYN, PIXELS), lambda: (0, 0)),
        out_shape=jax.ShapeDtypeStruct((SYN, PIXELS), BF),
        scratch_shapes=[buffer(s, t) for s, t in WEIGHTS + SAVED]
        + [
            buffer((SYN_ROWS, D), F32),
            buffer((SYN_ROWS, D), BF),
            buffer((SYN_ROWS, D), BF),
            buffer((SYN_ROWS, 3 * D), BF),
            buffer((SYN_ROWS, D), F32),
            buffer((SYN, D), F32),
            buffer((SYN // 8, 64, 384), F32),
            pltpu.SemaphoreType.DMA((9,)),
        ],
        compiler_params=pltpu.CompilerParams(vmem_limit_bytes=VMEM_LIMIT),
        cost_estimate=pl.CostEstimate(
            flops=4_000_000_000, bytes_accessed=12_000_000, transcendentals=0
        ),
        name="synth_backward",
    )(g, w, wp, *saved)


def gather_weights(core, x, patch_weight, qkv_weight, out_weight, images):
    columns = jnp.concatenate([qkv_weight, out_weight], axis=-1)
    patch = jnp.pad(patch_weight.reshape(2, 3, 2, 3, 128), ((0, 0),) * 3 + ((0, 1), (0, 0)))
    patch = patch.transpose(0, 1, 3, 2, 4).reshape(2, 12, 2, 128)
    both = jnp.concatenate([columns.reshape(2, 12, 2, 2 * D), patch], axis=-1)
    both = both.transpose(0, 2, 1, 3).reshape(4, 12, COLS)
    parts = []
    for k in range(4):
        to = (x - k) % 4
        first = to // 2 == core
        index = (to % 2) * 2 + jnp.where(first, 0, 1)

        def target(c, yy, zz, xx, k=k):
            to = (xx - k) % 4
            return (0, yy, zz, to) if to // 2 == c else (1, yy, zz, (to + 2) % 4)

        parts.append(permute(lax.dynamic_index_in_dim(both, index, 0, keepdims=False), target))
    ring = jnp.roll(jnp.stack(parts), x + 2 * core, axis=0).reshape(BLOCK_ROWS, COLS)
    near, far = (
        jnp.stack([ring, from_first(ring, 1)]),
        jnp.stack([from_first(ring, 2), from_first(ring, 3)]),
    )
    next_near, last_far = from_second(near, 1), from_second(far, 3)
    next_far, last_near = from_second(far, 1), from_second(near, 3)
    over_near, over_far = from_second(next_near, 1), from_second(last_far, 3)
    over_far, *images = lax.optimization_barrier((over_far, *images))
    mine = [near, far, next_near, next_far, over_near, over_far, last_near, last_far]
    theirs = [swap_cores(a) for a in mine]
    return mine, theirs, images


def local(
    real_images, real_labels, class_ids, synthetic, patch_weight, position, qkv_weight, out_weight
):
    core, img = lax.axis_index("enc"), lax.axis_index("img")
    y, z, x = img // 16, (img // 4) % 4, img % 4
    place = jnp.stack([core, y, z, x]).astype(jnp.int32)

    hit = real_labels[:, None] == class_ids[None, :]
    index = jnp.sum(jnp.where(hit, jnp.arange(64, dtype=F32)[None, :], 0.0), axis=1)
    tagged = jnp.concatenate(
        [real_images, jnp.broadcast_to(index[:, None], (64, 128)).astype(BF)], axis=1
    )
    syn = lax.dynamic_slice_in_dim(synthetic, 5 * core, 5, 0).astype(BF)
    images = jnp.concatenate(
        [lax.dynamic_slice_in_dim(tagged, 32 * core, 32, 0), jnp.pad(syn, ((0, 11), (0, 128)))],
        axis=0,
    )
    after = from_x(images, 1)
    images = [images, after, from_x(after, 1), from_x(images, 3)]
    their_pos = swap_cores(position)

    mine, theirs, images = gather_weights(
        core, x, patch_weight, qkv_weight, out_weight, images
    )
    csum, w, wp = run_real(place, position, their_pos, images, mine, theirs)

    groups = [[c * 64 + yz * 4 + xx for c in range(2) for yz in range(16)] for xx in range(4)]
    got = lax.all_to_all(csum, AXES, 0, 0, axis_index_groups=groups)
    total = jnp.sum(got.astype(F32), axis=0)
    means = total[:, :D] / jnp.maximum(total[:, D : D + 1], 1.0)

    own, *saved = run_synth(place, position, their_pos, images, w, wp)
    syn_mean = (own + swap_cores(own)) * (1.0 / IPC)
    g = (syn_mean - jnp.roll(means, -x, axis=0)) * (2.0 / (IPC * TOKENS))
    grads = run_back(g, w, wp, saved)

    sent = []
    for m in range(2):
        row = lax.dynamic_index_in_dim(means, (x - m) % 2 + 2 * core, 0, keepdims=True)
        sent.append(
            permute(row, lambda c, yy, zz, xx, m=m: (xx // 2, yy, zz, (xx - m) % 2 + 2 * c))
        )
    first = jnp.where(x % 2 == 0, sent[0], sent[1])
    second = jnp.where(x % 2 == 0, sent[1], sent[0])
    real_means = jnp.stack([first, second])

    grads = grads.reshape(4, SLOT, PIXELS)
    pixel = grads[0].astype(F32)
    for k in (1, 2, 3):
        pixel = pixel + from_x(grads[k], -k).astype(F32)
    pixel = pixel[:5]
    other = swap_cores(pixel)
    pixel_grad = jnp.concatenate(
        [jnp.where(core == 0, pixel, other), jnp.where(core == 0, other, pixel)], axis=0
    )
    return (real_means, pixel_grad)


def solution(mesh):
    return jax.shard_map(
        local,
        mesh=mesh,
        in_specs=(
            P("img", None),
            P("img"),
            P(),
            P("img", None),
            P("enc", "img", None),
            P("enc", None, None),
            P("enc", "img", None),
            P("enc", "img", None),
        ),
        out_specs=(P("enc", "img", None), P("img", None)),
        check_vma=False,
    )
```

```python
import jax
import jax.numpy as jnp
from jax import lax
from jax.experimental import pallas as pl
from jax.experimental.pallas import tpu as pltpu
from jax.sharding import PartitionSpec as P

AXES = ("enc", "img")
BF = jnp.bfloat16
F32 = jnp.float32
D = 768
PIXELS = 3072
IPC = 10
SLOT = 6
SYN = 4 * SLOT
BLOCK_ROWS = 48
COLS = 2 * D + 128
OUT_AT = COLS + D
STEP = 64
QKV_UNROLL = 9
SYN_QKV_UNROLL = 9
REAL = 128
TOKENS = 16
VMEM_LIMIT = 60 * 1024 * 1024


def flat(c, y, z, x):
    return (c % 2) * 64 + (y % 4) * 16 + (z % 4) * 4 + (x % 4)


PLACES = [(c, y, z, x) for c in range(2) for y in range(4) for z in range(4) for x in range(4)]


def permute(a, target):
    return lax.ppermute(a, AXES, [(flat(*p), flat(*target(*p))) for p in PLACES])


def swap_cores(a):
    return permute(a, lambda c, y, z, x: (1 - c, y, z, x))


def from_x(a, k):
    return permute(a, lambda c, y, z, x: (c, y, z, x - k))


def other_x(a):
    return permute(a, lambda c, y, z, x: (c, y, z, x ^ 1))


def across_x(a):
    return permute(a, lambda c, y, z, x: (c, y, z, 3 - x))


def other_second(a):
    return permute(a, lambda c, y, z, x: (c, y, z ^ 1, x) if c == 0 else (c, y ^ 1, z, x))


def across_second(a):
    return permute(a, lambda c, y, z, x: (c, y, 3 - z, x) if c == 0 else (c, 3 - y, z, x))


def ring_order(at):
    other = at + 1 - 2 * (at % 2)
    return (at, other, 3 - at, 3 - other)


def from_first(a, k):
    return permute(a, lambda c, y, z, x: (c, y - k, z, x) if c == 0 else (c, y, z - k, x))


def from_second(a, k):
    return permute(a, lambda c, y, z, x: (c, y, z - k, x) if c == 0 else (c, y - k, z, x))


def normalise(h):
    mean = jnp.mean(h, axis=-1, keepdims=True)
    centred = h - mean
    var = jnp.mean(centred * centred, axis=-1, keepdims=True)
    rstd = lax.rsqrt(var + 1e-06)
    return centred * rstd, rstd


def dot(a, b):
    return jnp.dot(a, b, preferred_element_type=F32)


def dot_nt(a, b):
    return lax.dot_general(a, b, (((1,), (1,)), ((), ())), preferred_element_type=F32)


def dot_tn(a, b):
    return lax.dot_general(a, b, (((0,), (0,)), ((), ())), preferred_element_type=F32)


def low_half():
    return lax.broadcasted_iota(jnp.int32, (128, 128), 1) < 64


def by_head(a, low):
    zero = jnp.zeros_like(a)
    return jnp.concatenate([jnp.where(low, a, zero), jnp.where(low, zero, a)], axis=0)


def image_bias():
    row = lax.broadcasted_iota(jnp.int32, (128, 128), 0)
    col = lax.broadcasted_iota(jnp.int32, (128, 128), 1)
    return jnp.where(row % 8 == col % 8, 0.0, -1e30).astype(F32)


def embed_rows(x32, wp_ref, tiles):
    halves = []
    for odd in range(2):
        rows = [
            x32[8 * t : 8 * t + 8, 384 * j + 128 * odd : 384 * j + 128 * odd + 256]
            for t in range(tiles)
            for j in range(8)
        ]
        halves.append(dot(jnp.concatenate(rows, axis=0).astype(BF), wp_ref[odd]))
    return [
        jnp.concatenate([h[64 * t : 64 * t + 64] for h in halves], axis=0) for t in range(tiles)
    ]


def exp_scores(s, bias):
    parts = []
    for h in range(2):
        sh = s[:, 128 * h : 128 * h + 128] + bias
        parts.append(jnp.exp(sh - jnp.max(sh, axis=-1, keepdims=True)))
    return parts


def pipeline(count, first, second, third):
    made = {}
    for k in range(count + 2):
        if k < count:
            made[k] = first(k)
        if 0 <= k - 2 < count:
            third(k - 2, *made.pop(k - 2))
        if 0 <= k - 1 < count:
            out = second(k - 1, made.pop(k - 1))
            made[k - 1] = () if out is None else (out,)


def loop(count, fn, unroll=1):
    def body(i, carry):
        fn(i)
        return carry

    lax.fori_loop(0, count, body, 0, unroll=unroll)


def mult(value, of):
    return value if isinstance(value, int) else pl.multiple_of(value, of)


def patch_sum(xhat):
    return jnp.sum(xhat.reshape(TOKENS, 8, D), axis=0) * (1.0 / TOKENS)


def qkv_product(n_ref, w_ref, qkv_ref, unroll):
    def chunk(c):
        at = mult(256 * c, 128)
        col = mult(256 * c + jnp.where(c >= 6, 128, 0), 128)
        out = dot(n_ref[...], w_ref[:, pl.ds(col, 256)])
        qkv_ref[:, pl.ds(at, 256)] = (out * jnp.where(c < 3, 0.125, 1.0)).astype(BF)

    loop(9, chunk, unroll)


def out_product(att_ref, w_ref, e_ref):
    def chunk(c):
        at = mult(256 * c, 128)
        e_ref[:, pl.ds(at, 256)] += dot(att_ref[...], w_ref[:, pl.ds(OUT_AT + at, 256)])

    loop(3, chunk, 3)


def spread_position(where_ref, mine_ref, theirs_ref, posx_ref):
    core, x = where_ref[0], where_ref[3]
    local = x // 2 == core
    pos = jnp.where(local, mine_ref[lax.rem(x, 2)], theirs_ref[lax.rem(x, 2)]).astype(F32)
    for patch in range(TOKENS):
        at = (patch % 2) * 64 + (patch // 2) * 8
        posx_ref[at : at + 8] = jnp.broadcast_to(pos[patch : patch + 1], (8, D))


def real_kernel(
    where_ref, mine_ref, theirs_ref, images_ref, l0, l1, l2, l3, o0, o1, o2, o3,
    csum_ref, w_out, wp_out,
    e_ref, n_ref, qkv_ref, att_ref, feat_ref, hot_ref, x_ref, posx_ref, w_ref, wp_ref, sems,
):
    tiles = STEP // 8
    groups = REAL // STEP
    core, y, z = where_ref[0], where_ref[1], where_ref[2]

    for k in range(4):
        pltpu.make_async_copy(
            images_ref.at[k, 0:32], x_ref.at[32 * k : 32 * k + 32], sems.at[1]
        ).start()
    near_block = ((0, 0), (0, 1), (1, 0), (1, 1))
    far_block = ((2, 0), (3, 0), (2, 1), (3, 1))
    for cols, sem in ((pl.ds(2 * D, 128), 0), (pl.ds(0, 2 * D), 4)):
        for other, refs in enumerate(((l0, l1, l2, l3), (o0, o1, o2, o3))):
            part = lax.rem(core + other, 2)
            first, second = jnp.where(part == 0, y, z), jnp.where(part == 0, z, y)
            target = pl.ds(pl.multiple_of(part * COLS + cols.start, 128), cols.size)
            for j, at in enumerate(ring_order(second)):
                for i in range(4):
                    line = lax.rem(first + i, 4)
                    block = jnp.where(part == 0, line * 4 + at, at * 4 + line)
                    row = pl.multiple_of(block * BLOCK_ROWS, 16)
                    ref, index = (near_block if i < 2 else far_block)[j]
                    pltpu.make_async_copy(
                        refs[ref].at[index, i % 2, :, cols],
                        w_ref.at[pl.ds(row, BLOCK_ROWS), target],
                        sems.at[sem],
                    ).start()
    wp_ref[...] = jnp.zeros_like(wp_ref)
    spread_position(where_ref, mine_ref, theirs_ref, posx_ref)
    cls = lax.broadcasted_iota(jnp.int32, (REAL, 128), 1).astype(F32)
    pltpu.make_async_copy(x_ref, x_ref, sems.at[1]).wait()
    hot_ref[...] = jnp.where(x_ref[:, PIXELS:].astype(F32) == cls, 1.0, 0.0).astype(BF)
    feat_ref[:, D:] = jnp.ones((REAL, 128), BF)
    patch_cols = w_ref.at[:, : 2 * 128]
    pltpu.make_async_copy(patch_cols, patch_cols, sems.at[0]).wait()
    out_row = lax.broadcasted_iota(jnp.int32, (192, D), 0)
    in_row = lax.broadcasted_iota(jnp.int32, (192, D), 1)

    def decode(j):
        pick = jnp.where(in_row == 4 * out_row + j, 1.0, 0.0).astype(BF)
        for part in range(2):
            piece = dot(pick, w_ref[:, part * COLS + 2 * D : (part + 1) * COLS]).astype(BF)
            at = mult(384 * part + 128 * j, 128)
            wp_ref[0, 0:192, pl.ds(at, 128)] = piece
            wp_ref[1, 64:256, pl.ds(at, 128)] = piece

    loop(3, decode, 3)
    save_wp = pltpu.make_async_copy(wp_ref, wp_out, sems.at[3])
    save_wp.start()

    def embed(g):
        at = mult(g * STEP, STEP)
        x32 = x_ref[pl.ds(at, STEP), :PIXELS].astype(F32)
        for t, e in enumerate(embed_rows(x32, wp_ref, tiles)):
            e = e + posx_ref[...]
            e_ref[g, 128 * t : 128 * t + 128] = e
            n_ref[g, 128 * t : 128 * t + 128] = normalise(e)[0].astype(BF)

    loop(groups, embed)
    main_cols = w_ref.at[:, : 4 * D]
    pltpu.make_async_copy(main_cols, main_cols, sems.at[4]).wait()
    save_w = pltpu.make_async_copy(w_ref, w_out, sems.at[2])
    save_w.start()
    low = low_half()
    bias = image_bias()
    ones = by_head(jnp.ones((128, 128), BF), low)

    def score(u):
        rows = pl.ds((u // 6) * 128, 128)
        at = (u % 6) * 128
        kbd = by_head(qkv_ref[rows, D + at : D + at + 128], low)
        return dot_nt(qkv_ref[rows, at : at + 128], kbd)

    def soften(u, s):
        return jnp.concatenate(exp_scores(s, bias), axis=1).astype(BF)

    def weigh(u, ex):
        rows = pl.ds((u // 6) * 128, 128)
        at = (u % 6) * 128
        vbd = by_head(qkv_ref[rows, 2 * D + at : 2 * D + at + 128], low)
        o = dot(ex, jnp.concatenate([vbd, ones], axis=1))
        att_ref[rows, at : at + 128] = (o[:, :128] / o[:, 128:]).astype(BF)

    def group(g):
        at = mult(g * STEP, STEP)
        qkv_product(n_ref.at[g], w_ref, qkv_ref, QKV_UNROLL)
        pipeline(6 * tiles, score, soften, weigh)
        out_product(att_ref, w_ref, e_ref.at[g])
        feats = [patch_sum(normalise(e_ref[g, 128 * t : 128 * t + 128])[0]) for t in range(tiles)]
        feat_ref[pl.ds(at, STEP), :D] = jnp.concatenate(feats, axis=0).astype(BF)

    loop(groups, group)
    sums = dot_tn(hot_ref[...], feat_ref[...])
    for b in range(16):
        block = sums[4 * b : 4 * b + 4].astype(csum_ref.dtype)
        csum_ref[b] = block
        csum_ref[16 + b] = block
    save_w.wait()
    save_wp.wait()


def copies_of(pairs, sems):
    copies = [pltpu.make_async_copy(src, dst, sems.at[i]) for i, (src, dst) in enumerate(pairs)]
    for copy in copies:
        copy.start()
    return copies


def synth_kernel(
    where_ref, mine_ref, theirs_ref, images_ref, w_in, wp_in,
    sum_ref, n_out, r1_out, qkv_out, p_out, xhat2_out, r2_out,
    n_ref, r1_ref, qkv_ref, p_ref, xhat2_ref, r2_ref,
    e_ref, att_ref, x_ref, posx_ref, w_ref, wp_ref, in_sems, sems,
):
    tiles = SYN // 8
    pairs = [
        (images_ref.at[k, 32:48, :PIXELS], x_ref.at[16 * k : 16 * k + 16])
        for k in range(4)
    ]
    loads = copies_of(pairs + [(wp_in, wp_ref), (w_in, w_ref)], in_sems)
    saves = [
        pltpu.make_async_copy(src, dst, sems.at[i])
        for i, (src, dst) in enumerate(
            (
                (n_ref, n_out), (r1_ref, r1_out), (qkv_ref, qkv_out),
                (p_ref, p_out), (xhat2_ref, xhat2_out), (r2_ref, r2_out),
            )
        )
    ]
    spread_position(where_ref, mine_ref, theirs_ref, posx_ref)
    for copy in loads[:5]:
        copy.wait()
    x32 = jnp.concatenate([x_ref[16 * k : 16 * k + 16].astype(F32)[:SLOT] for k in range(4)], axis=0)
    for t, e in enumerate(embed_rows(x32, wp_ref, tiles)):
        rows = slice(128 * t, 128 * t + 128)
        e = e + posx_ref[...]
        e_ref[rows] = e
        xhat, rstd = normalise(e)
        r1_ref[rows] = jnp.broadcast_to(rstd, (128, 128))
        n_ref[rows] = xhat.astype(BF)
    saves[0].start()
    saves[1].start()
    loads[5].wait()
    qkv_product(n_ref, w_ref, qkv_ref, SYN_QKV_UNROLL)
    saves[2].start()
    low = low_half()
    bias = image_bias()

    def score(u):
        rows, at = pl.ds((u // 6) * 128, 128), (u % 6) * 128
        kbd = by_head(qkv_ref[rows, D + at : D + at + 128], low)
        return dot_nt(qkv_ref[rows, at : at + 128], kbd)

    def soften(u, s):
        rows, at = pl.ds((u // 6) * 128, 128), (u % 6) * 256
        parts = [ex / jnp.sum(ex, axis=-1, keepdims=True) for ex in exp_scores(s, bias)]
        p_ref[rows, at : at + 256] = jnp.concatenate(parts, axis=1).astype(BF)

    def weigh(u):
        rows, at = pl.ds((u // 6) * 128, 128), (u % 6) * 128
        vbd = by_head(qkv_ref[rows, 2 * D + at : 2 * D + at + 128], low)
        att_ref[rows, at : at + 128] = dot(p_ref[rows, 2 * at : 2 * at + 256], vbd).astype(BF)

    pipeline(6 * tiles, score, soften, weigh)
    saves[3].start()
    out_product(att_ref, w_ref, e_ref)
    feats = []
    for t in range(tiles):
        rows = slice(128 * t, 128 * t + 128)
        xhat, rstd = normalise(e_ref[rows])
        xhat2_ref[rows] = xhat.astype(BF)
        r2_ref[rows] = jnp.broadcast_to(rstd, (128, 128))
        feats.append(patch_sum(xhat))
    saves[4].start()
    saves[5].start()
    feats = jnp.concatenate(feats, axis=0)
    for s in range(4):
        sum_ref[s : s + 1] = jnp.sum(feats[SLOT * s : SLOT * s + 5], axis=0, keepdims=True)
    for copy in saves:
        copy.wait()


def norm_back(g, xhat, rstd):
    mean_g = jnp.mean(g, axis=-1, keepdims=True)
    mean_gx = jnp.mean(g * xhat, axis=-1, keepdims=True)
    return rstd[:, :1] * (g - mean_g - xhat * mean_gx)


def back_kernel(
    where_ref, means_ref, own_ref, their_ref, w_in, wp_in, n_in, r1_in, qkv_in, p_in, xhat2_in, r2_in,
    out0, out1, out2, out3,
    w_ref, wp_ref, n_ref, r1_ref, qkv_ref, p_ref, xhat2_ref, r2_ref,
    dh_ref, dhb_ref, da_ref, dqkv_ref, dn_ref, spread_ref, px_ref, grad_ref, sems,
):
    tiles = SYN // 8
    out_cols = pl.ds(OUT_AT, D)
    loads = copies_of(
        (
            (xhat2_in, xhat2_ref), (r2_in, r2_ref),
            (w_in.at[:, out_cols], w_ref.at[:, out_cols]),
            (qkv_in, qkv_ref), (p_in, p_ref),
            (w_in.at[:, :OUT_AT], w_ref.at[:, :OUT_AT]),
            (n_in, n_ref), (r1_in, r1_ref), (wp_in, wp_ref),
        ),
        sems,
    )
    image = lax.broadcasted_iota(jnp.int32, (SYN, D), 0)
    spread = jnp.zeros((SYN, D), F32)
    for s in range(4):
        mine = (image >= SLOT * s) & (image < SLOT * s + 5)
        syn = (own_ref[s : s + 1] + their_ref[s : s + 1]) * (1.0 / IPC)
        g = (syn - means_ref[s : s + 1]) * (2.0 / (IPC * TOKENS))
        spread = jnp.where(mine, g, spread)
    spread_ref[...] = spread
    loads[0].wait()
    loads[1].wait()

    def second_norm(t):
        rows = pl.ds(mult(128 * t, 128), 128)
        g = spread_ref[pl.ds(mult(8 * t, 8), 8)]
        g = jnp.broadcast_to(g[None], (TOKENS, 8, D)).reshape(128, D)
        dh = norm_back(g, xhat2_ref[rows].astype(F32), r2_ref[rows])
        dh_ref[rows] = dh
        dhb_ref[rows] = dh.astype(BF)

    loop(tiles, second_norm, tiles)
    loads[2].wait()

    def out_back(c):
        at = mult(256 * c, 128)
        da_ref[:, pl.ds(at, 256)] = dot_nt(
            dhb_ref[...], w_ref[pl.ds(at, 256), OUT_AT : OUT_AT + D]
        ).astype(BF)

    loop(3, out_back, 3)
    loads[3].wait()
    loads[4].wait()
    low = low_half()

    def probs_back(u):
        rows, at = pl.ds((u // 6) * 128, 128), (u % 6) * 128
        da = da_ref[rows, at : at + 128]
        return dot_nt(da, by_head(qkv_ref[rows, 2 * D + at : 2 * D + at + 128], low))

    def scores_back(u, dp):
        rows, at = pl.ds((u // 6) * 128, 128), (u % 6) * 128
        da = da_ref[rows, at : at + 128]
        probs = p_ref[rows, 2 * at : 2 * at + 256]
        dv = dot_tn(probs, da)
        dqkv_ref[rows, 2 * D + at : 2 * D + at + 128] = jnp.where(low, dv[:128], dv[128:]).astype(BF)
        p32 = probs.astype(F32)
        ds = []
        for h in range(2):
            ph, dph = p32[:, 128 * h : 128 * h + 128], dp[:, 128 * h : 128 * h + 128]
            inner = jnp.sum(ph * dph, axis=-1, keepdims=True)
            ds.append(ph * (dph - inner))
        return jnp.concatenate(ds, axis=1).astype(BF)

    def query_key_back(u, ds):
        rows, at = pl.ds((u // 6) * 128, 128), (u % 6) * 128
        kbd = by_head(qkv_ref[rows, D + at : D + at + 128], low)
        dqkv_ref[rows, at : at + 128] = (dot(ds, kbd) * 0.125).astype(BF)
        dk = dot_tn(ds, qkv_ref[rows, at : at + 128])
        dqkv_ref[rows, D + at : D + at + 128] = jnp.where(low, dk[:128], dk[128:]).astype(BF)

    pipeline(6 * tiles, probs_back, scores_back, query_key_back)
    loads[5].wait()

    def qkv_back(c):
        at = mult(256 * c, 128)
        rows = pl.ds(at, 256)
        dn = dot_nt(dqkv_ref[:, : 2 * D], w_ref[rows, : 2 * D])
        dn_ref[:, rows] = dn + dot_nt(dqkv_ref[:, 2 * D :], w_ref[rows, COLS : COLS + D])

    loop(3, qkv_back, 3)
    for copy in loads[6:]:
        copy.wait()

    def first_norm(t):
        rows = pl.ds(mult(128 * t, 128), 128)
        de = dh_ref[rows] + norm_back(dn_ref[rows], n_ref[rows].astype(F32), r1_ref[rows])
        de = de.astype(BF)
        even = dot_nt(de[:64], wp_ref[0])
        odd = dot_nt(de[64:], wp_ref[1])
        px_ref[t] = jnp.concatenate(
            [even[:, :128], even[:, 128:] + odd[:, :128], odd[:, 128:]], axis=1
        )

    loop(tiles, first_norm, tiles)
    for j in range(8):
        cols = slice(384 * j, 384 * j + 384)
        all_rows = jnp.concatenate([px_ref[t, 8 * j : 8 * j + 8] for t in range(tiles)], axis=0)
        for s in range(4):
            grad_ref[8 * s : 8 * s + SLOT, cols] = all_rows[SLOT * s : SLOT * s + SLOT]
    for at, out in zip(ring_order(where_ref[3]), (out0, out1, out2, out3)):
        out[...] = grad_ref[pl.ds(mult(8 * at, 8), 8)][:5].astype(BF)


SMEM_SPEC = pl.BlockSpec(memory_space=pltpu.SMEM)
VMEM_SPEC = pl.BlockSpec(memory_space=pltpu.VMEM)
ANY_SPEC = pl.BlockSpec(memory_space=pltpu.HBM)


def buffer(shape, kind):
    return pltpu.VMEM(shape, kind)


def run_real(place, mine_pos, their_pos, images, mine, theirs):
    rows = STEP * TOKENS
    return pl.pallas_call(
        real_kernel,
        in_specs=[SMEM_SPEC, VMEM_SPEC, VMEM_SPEC] + [ANY_SPEC] * 9,
        out_specs=[pl.BlockSpec((32, 4, D + 128), lambda: (0, 0, 0)), ANY_SPEC, ANY_SPEC],
        out_shape=[
            jax.ShapeDtypeStruct((32, 4, D + 128), BF),
            jax.ShapeDtypeStruct((D, 2 * COLS), BF),
            jax.ShapeDtypeStruct((2, 256, D), BF),
        ],
        scratch_shapes=[
            buffer((REAL // STEP, rows, D), F32),
            buffer((REAL // STEP, rows, D), BF),
            buffer((rows, 3 * D), BF),
            buffer((rows, D), BF),
            buffer((REAL, D + 128), BF),
            buffer((REAL, 128), BF),
            buffer((REAL, PIXELS + 128), BF),
            buffer((128, D), F32),
            buffer((D, 2 * COLS), BF),
            buffer((2, 256, D), BF),
            pltpu.SemaphoreType.DMA((5,)),
        ],
        compiler_params=pltpu.CompilerParams(vmem_limit_bytes=VMEM_LIMIT),
        cost_estimate=pl.CostEstimate(
            flops=14_000_000_000, bytes_accessed=12_000_000, transcendentals=3_000_000
        ),
        name="real_forward",
    )(place, mine_pos, their_pos, images, *mine, *theirs)


SYN_ROWS = SYN * TOKENS
SAVED = [
    ((SYN_ROWS, D), BF),
    ((SYN_ROWS, 128), F32),
    ((SYN_ROWS, 3 * D), BF),
    ((SYN_ROWS, 2 * D), BF),
    ((SYN_ROWS, D), BF),
    ((SYN_ROWS, 128), F32),
]
WEIGHTS = [((D, 2 * COLS), BF), ((2, 256, D), BF)]


def run_synth(place, mine_pos, their_pos, images, w, wp):
    return pl.pallas_call(
        synth_kernel,
        in_specs=[SMEM_SPEC, VMEM_SPEC, VMEM_SPEC] + [ANY_SPEC] * 3,
        out_specs=[pl.BlockSpec((4, D), lambda: (0, 0))] + [ANY_SPEC] * 6,
        out_shape=[jax.ShapeDtypeStruct((4, D), F32)]
        + [jax.ShapeDtypeStruct(s, t) for s, t in SAVED],
        scratch_shapes=[buffer(s, t) for s, t in SAVED]
        + [
            buffer((SYN_ROWS, D), F32),
            buffer((SYN_ROWS, D), BF),
            buffer((64, PIXELS), BF),
            buffer((128, D), F32),
        ]
        + [buffer(s, t) for s, t in WEIGHTS]
        + [pltpu.SemaphoreType.DMA((6,)), pltpu.SemaphoreType.DMA((6,))],
        compiler_params=pltpu.CompilerParams(vmem_limit_bytes=VMEM_LIMIT),
        cost_estimate=pl.CostEstimate(
            flops=3_000_000_000, bytes_accessed=12_000_000, transcendentals=600_000
        ),
        name="synth_forward",
    )(place, mine_pos, their_pos, images, w, wp)


def run_back(place, means, own, their, w, wp, saved):
    return pl.pallas_call(
        back_kernel,
        in_specs=[SMEM_SPEC] + [VMEM_SPEC] * 3 + [ANY_SPEC] * 8,
        out_specs=[pl.BlockSpec((5, PIXELS), lambda: (0, 0))] * 4,
        out_shape=[jax.ShapeDtypeStruct((5, PIXELS), BF)] * 4,
        scratch_shapes=[buffer(s, t) for s, t in WEIGHTS + SAVED]
        + [
            buffer((SYN_ROWS, D), F32),
            buffer((SYN_ROWS, D), BF),
            buffer((SYN_ROWS, D), BF),
            buffer((SYN_ROWS, 3 * D), BF),
            buffer((SYN_ROWS, D), F32),
            buffer((SYN, D), F32),
            buffer((SYN // 8, 64, 384), F32),
            buffer((32, PIXELS), F32),
            pltpu.SemaphoreType.DMA((9,)),
        ],
        compiler_params=pltpu.CompilerParams(vmem_limit_bytes=VMEM_LIMIT),
        cost_estimate=pl.CostEstimate(
            flops=4_000_000_000, bytes_accessed=12_000_000, transcendentals=0
        ),
        name="synth_backward",
    )(place, means, own, their, w, wp, *saved)


def gather_weights(core, x, patch_weight, qkv_weight, out_weight, images):
    columns = jnp.concatenate([qkv_weight, out_weight], axis=-1)
    patch = jnp.pad(patch_weight.reshape(2, 3, 2, 3, 128), ((0, 0),) * 3 + ((0, 1), (0, 0)))
    patch = patch.transpose(0, 1, 3, 2, 4).reshape(2, 12, 2, 128)
    both = jnp.concatenate([columns.reshape(2, 12, 2, 2 * D), patch], axis=-1)
    both = both.transpose(0, 2, 1, 3).reshape(4, 12, COLS)
    parts = []
    for k in range(4):
        to = (x - k) % 4
        first = to // 2 == core
        index = (to % 2) * 2 + jnp.where(first, 0, 1)

        def target(c, yy, zz, xx, k=k):
            to = (xx - k) % 4
            return (0, yy, zz, to) if to // 2 == c else (1, yy, zz, (to + 2) % 4)

        parts.append(permute(lax.dynamic_index_in_dim(both, index, 0, keepdims=False), target))
    ring = jnp.roll(jnp.stack(parts), x + 2 * core, axis=0).reshape(BLOCK_ROWS, COLS)
    near, far = (
        jnp.stack([ring, from_first(ring, 1)]),
        jnp.stack([from_first(ring, 2), from_first(ring, 3)]),
    )
    near = jnp.stack([near, other_second(near)])
    far = jnp.stack([far, across_second(far)])
    near_across, far_other = across_second(near), other_second(far)
    near_across, images, their_pos = lax.optimization_barrier((near_across, *images))
    mine = [near, near_across, far, far_other]
    theirs = [swap_cores(a) for a in mine]
    return mine, theirs, images, their_pos


def local(
    real_images, real_labels, class_ids, synthetic, patch_weight, position, qkv_weight, out_weight
):
    core, img = lax.axis_index("enc"), lax.axis_index("img")
    y, z, x = img // 16, (img // 4) % 4, img % 4
    place = jnp.stack([core, y, z, x]).astype(jnp.int32)

    hit = real_labels[:, None] == class_ids[None, :]
    index = jnp.sum(jnp.where(hit, jnp.arange(64, dtype=F32)[None, :], 0.0), axis=1)
    tagged = jnp.concatenate(
        [real_images, jnp.broadcast_to(index[:, None], (64, 128)).astype(BF)], axis=1
    )
    syn = lax.dynamic_slice_in_dim(synthetic, 5 * core, 5, 0).astype(BF)
    images = jnp.concatenate(
        [lax.dynamic_slice_in_dim(tagged, 32 * core, 32, 0), jnp.pad(syn, ((0, 11), (0, 128)))],
        axis=0,
    )
    rings = [[flat(c, yz // 4, yz % 4, xx) for xx in range(4)] for c in range(2) for yz in range(16)]
    images = lax.all_to_all(
        jnp.broadcast_to(images[None], (4, 48, PIXELS + 128)), AXES, 0, 0, axis_index_groups=rings
    )
    images = (images, swap_cores(position))
    mine, theirs, images, their_pos = gather_weights(
        core, x, patch_weight, qkv_weight, out_weight, images
    )
    csum, w, wp = run_real(place, position, their_pos, images, mine, theirs)

    groups = [[c * 64 + yz * 4 + xx for c in range(2) for yz in range(16)] for xx in range(4)]
    got = lax.all_to_all(csum, AXES, 0, 0, axis_index_groups=groups)
    total = jnp.sum(got.astype(F32), axis=0)
    means = total[:, :D] / jnp.maximum(total[:, D : D + 1], 1.0)

    own, *saved = run_synth(place, position, their_pos, images, w, wp)
    grads = run_back(place, means, own, swap_cores(own), w, wp, saved)

    means, grads = lax.optimization_barrier((means, grads))
    sent = []
    for m in range(2):
        row = lax.dynamic_index_in_dim(means, (x - m) % 2 + 2 * core, 0, keepdims=True)
        sent.append(
            permute(row, lambda c, yy, zz, xx, m=m: (xx // 2, yy, zz, (xx - m) % 2 + 2 * c))
        )
    first = jnp.where(x % 2 == 0, sent[0], sent[1])
    second = jnp.where(x % 2 == 0, sent[1], sent[0])
    real_means = jnp.stack([first, second])

    pixel = grads[0].astype(F32) + other_x(grads[1]).astype(F32)
    pixel = pixel + across_x(grads[2]).astype(F32) + from_x(grads[3], 2).astype(F32)
    other = swap_cores(pixel)
    pixel_grad = jnp.concatenate(
        [jnp.where(core == 0, pixel, other), jnp.where(core == 0, other, pixel)], axis=0
    )
    return (real_means, pixel_grad)


def solution(mesh):
    return jax.shard_map(
        local,
        mesh=mesh,
        in_specs=(
            P("img", None),
            P("img"),
            P(),
            P("img", None),
            P("enc", "img", None),
            P("enc", None, None),
            P("enc", "img", None),
            P("enc", "img", None),
        ),
        out_specs=(P("enc", "img", None), P("img", None)),
        check_vma=False,
    )
```

```python
import jax
import jax.numpy as jnp
from jax import lax
from jax.experimental import pallas as pl
from jax.experimental.pallas import tpu as pltpu
from jax.sharding import PartitionSpec as P

AXES = ("enc", "img")
BF = jnp.bfloat16
F32 = jnp.float32
D = 768
PIXELS = 3072
IPC = 10
SYN_AT = PIXELS + 128
SLOT = 6
SYN = 4 * SLOT
BLOCK_ROWS = 48
COLS = 2 * D + 128
OUT_AT = COLS + D
STEP = 64
QKV_UNROLL = 9
SYN_QKV_UNROLL = 9
REAL = 128
TOKENS = 16
VMEM_LIMIT = 60 * 1024 * 1024


def flat(c, y, z, x):
    return (c % 2) * 64 + (y % 4) * 16 + (z % 4) * 4 + (x % 4)


PLACES = [(c, y, z, x) for c in range(2) for y in range(4) for z in range(4) for x in range(4)]


def permute(a, target):
    return lax.ppermute(a, AXES, [(flat(*p), flat(*target(*p))) for p in PLACES])


def swap_cores(a):
    return permute(a, lambda c, y, z, x: (1 - c, y, z, x))


def from_x(a, k):
    return permute(a, lambda c, y, z, x: (c, y, z, x - k))


def other_x(a):
    return permute(a, lambda c, y, z, x: (c, y, z, x ^ 1))


def across_x(a):
    return permute(a, lambda c, y, z, x: (c, y, z, 3 - x))


def other_second(a):
    return permute(a, lambda c, y, z, x: (c, y, z ^ 1, x) if c == 0 else (c, y ^ 1, z, x))


def across_second(a):
    return permute(a, lambda c, y, z, x: (c, y, 3 - z, x) if c == 0 else (c, 3 - y, z, x))


def ring_order(at):
    other = at + 1 - 2 * (at % 2)
    return (at, other, 3 - at, 3 - other)


def from_first(a, k):
    return permute(a, lambda c, y, z, x: (c, y - k, z, x) if c == 0 else (c, y, z - k, x))


def from_second(a, k):
    return permute(a, lambda c, y, z, x: (c, y, z - k, x) if c == 0 else (c, y - k, z, x))


def normalise(h):
    mean = jnp.mean(h, axis=-1, keepdims=True)
    centred = h - mean
    var = jnp.mean(centred * centred, axis=-1, keepdims=True)
    rstd = lax.rsqrt(var + 1e-06)
    return centred * rstd, rstd


def dot(a, b):
    return jnp.dot(a, b, preferred_element_type=F32)


def dot_nt(a, b):
    return lax.dot_general(a, b, (((1,), (1,)), ((), ())), preferred_element_type=F32)


def dot_tn(a, b):
    return lax.dot_general(a, b, (((0,), (0,)), ((), ())), preferred_element_type=F32)


def low_half():
    return lax.broadcasted_iota(jnp.int32, (128, 128), 1) < 64


def by_head(a, low):
    zero = jnp.zeros_like(a)
    return jnp.concatenate([jnp.where(low, a, zero), jnp.where(low, zero, a)], axis=0)


def image_bias():
    row = lax.broadcasted_iota(jnp.int32, (128, 128), 0)
    col = lax.broadcasted_iota(jnp.int32, (128, 128), 1)
    return jnp.where(row % 8 == col % 8, 0.0, -1e30).astype(F32)


def embed_rows(x32, wp_ref, tiles):
    halves = []
    for odd in range(2):
        rows = [
            x32[8 * t : 8 * t + 8, 384 * j + 128 * odd : 384 * j + 128 * odd + 256]
            for t in range(tiles)
            for j in range(8)
        ]
        halves.append(dot(jnp.concatenate(rows, axis=0).astype(BF), wp_ref[odd]))
    return [
        jnp.concatenate([h[64 * t : 64 * t + 64] for h in halves], axis=0) for t in range(tiles)
    ]


def exp_scores(s, bias):
    parts = []
    for h in range(2):
        sh = s[:, 128 * h : 128 * h + 128] + bias
        parts.append(jnp.exp(sh - jnp.max(sh, axis=-1, keepdims=True)))
    return parts


def pipeline(count, first, second, third):
    made = {}
    for k in range(count + 2):
        if k < count:
            made[k] = first(k)
        if 0 <= k - 2 < count:
            third(k - 2, *made.pop(k - 2))
        if 0 <= k - 1 < count:
            out = second(k - 1, made.pop(k - 1))
            made[k - 1] = () if out is None else (out,)


def loop(count, fn, unroll=1):
    def body(i, carry):
        fn(i)
        return carry

    lax.fori_loop(0, count, body, 0, unroll=unroll)


def mult(value, of):
    return value if isinstance(value, int) else pl.multiple_of(value, of)


def patch_sum(xhat):
    return jnp.sum(xhat.reshape(TOKENS, 8, D), axis=0) * (1.0 / TOKENS)


def qkv_product(n_ref, w_ref, qkv_ref, unroll):
    def chunk(c):
        at = mult(256 * c, 128)
        col = mult(256 * c + jnp.where(c >= 6, 128, 0), 128)
        out = dot(n_ref[...], w_ref[:, pl.ds(col, 256)])
        qkv_ref[:, pl.ds(at, 256)] = (out * jnp.where(c < 3, 0.125, 1.0)).astype(BF)

    loop(9, chunk, unroll)


def out_product(att_ref, w_ref, e_ref):
    def chunk(c):
        at = mult(256 * c, 128)
        e_ref[:, pl.ds(at, 256)] += dot(att_ref[...], w_ref[:, pl.ds(OUT_AT + at, 256)])

    loop(3, chunk, 3)


def spread_position(where_ref, mine_ref, theirs_ref, posx_ref):
    core, x = where_ref[0], where_ref[3]
    local = x // 2 == core
    pos = jnp.where(local, mine_ref[lax.rem(x, 2)], theirs_ref[lax.rem(x, 2)]).astype(F32)
    for patch in range(TOKENS):
        at = (patch % 2) * 64 + (patch // 2) * 8
        posx_ref[at : at + 8] = jnp.broadcast_to(pos[patch : patch + 1], (8, D))


def real_kernel(
    where_ref, mine_ref, theirs_ref, images_ref, l0, l1, l2, l3, o0, o1, o2, o3,
    csum_ref, w_out, wp_out,
    e_ref, n_ref, qkv_ref, att_ref, feat_ref, hot_ref, x_ref, posx_ref, w_ref, wp_ref, sems,
):
    tiles = STEP // 8
    groups = REAL // STEP
    core, y, z = where_ref[0], where_ref[1], where_ref[2]

    for k in range(4):
        pltpu.make_async_copy(
            images_ref.at[k, :, :SYN_AT], x_ref.at[32 * k : 32 * k + 32], sems.at[1]
        ).start()
    near_block = ((0, 0), (0, 1), (1, 0), (1, 1))
    far_block = ((2, 0), (3, 0), (2, 1), (3, 1))
    for cols, sem in ((pl.ds(2 * D, 128), 0), (pl.ds(0, 2 * D), 4)):
        for other, refs in enumerate(((l0, l1, l2, l3), (o0, o1, o2, o3))):
            part = lax.rem(core + other, 2)
            first, second = jnp.where(part == 0, y, z), jnp.where(part == 0, z, y)
            target = pl.ds(pl.multiple_of(part * COLS + cols.start, 128), cols.size)
            for j, at in enumerate(ring_order(second)):
                for i in range(4):
                    line = lax.rem(first + i, 4)
                    block = jnp.where(part == 0, line * 4 + at, at * 4 + line)
                    row = pl.multiple_of(block * BLOCK_ROWS, 16)
                    ref, index = (near_block if i < 2 else far_block)[j]
                    pltpu.make_async_copy(
                        refs[ref].at[index, i % 2, :, cols],
                        w_ref.at[pl.ds(row, BLOCK_ROWS), target],
                        sems.at[sem],
                    ).start()
    wp_ref[...] = jnp.zeros_like(wp_ref)
    spread_position(where_ref, mine_ref, theirs_ref, posx_ref)
    cls = lax.broadcasted_iota(jnp.int32, (REAL, 128), 1).astype(F32)
    pltpu.make_async_copy(x_ref, x_ref, sems.at[1]).wait()
    hot_ref[...] = jnp.where(x_ref[:, PIXELS:].astype(F32) == cls, 1.0, 0.0).astype(BF)
    feat_ref[:, D:] = jnp.ones((REAL, 128), BF)
    patch_cols = w_ref.at[:, : 2 * 128]
    pltpu.make_async_copy(patch_cols, patch_cols, sems.at[0]).wait()
    out_row = lax.broadcasted_iota(jnp.int32, (192, D), 0)
    in_row = lax.broadcasted_iota(jnp.int32, (192, D), 1)

    def decode(j):
        pick = jnp.where(in_row == 4 * out_row + j, 1.0, 0.0).astype(BF)
        for part in range(2):
            piece = dot(pick, w_ref[:, part * COLS + 2 * D : (part + 1) * COLS]).astype(BF)
            at = mult(384 * part + 128 * j, 128)
            wp_ref[0, 0:192, pl.ds(at, 128)] = piece
            wp_ref[1, 64:256, pl.ds(at, 128)] = piece

    loop(3, decode, 3)
    save_wp = pltpu.make_async_copy(wp_ref, wp_out, sems.at[3])
    save_wp.start()

    def embed(g):
        at = mult(g * STEP, STEP)
        x32 = x_ref[pl.ds(at, STEP), :PIXELS].astype(F32)
        for t, e in enumerate(embed_rows(x32, wp_ref, tiles)):
            e = e + posx_ref[...]
            e_ref[g, 128 * t : 128 * t + 128] = e
            n_ref[g, 128 * t : 128 * t + 128] = normalise(e)[0].astype(BF)

    loop(groups, embed)
    main_cols = w_ref.at[:, : 4 * D]
    pltpu.make_async_copy(main_cols, main_cols, sems.at[4]).wait()
    save_w = pltpu.make_async_copy(w_ref, w_out, sems.at[2])
    save_w.start()
    low = low_half()
    bias = image_bias()
    ones = by_head(jnp.ones((128, 128), BF), low)

    def score(u):
        rows = pl.ds((u // 6) * 128, 128)
        at = (u % 6) * 128
        kbd = by_head(qkv_ref[rows, D + at : D + at + 128], low)
        return dot_nt(qkv_ref[rows, at : at + 128], kbd)

    def soften(u, s):
        return jnp.concatenate(exp_scores(s, bias), axis=1).astype(BF)

    def weigh(u, ex):
        rows = pl.ds((u // 6) * 128, 128)
        at = (u % 6) * 128
        vbd = by_head(qkv_ref[rows, 2 * D + at : 2 * D + at + 128], low)
        o = dot(ex, jnp.concatenate([vbd, ones], axis=1))
        att_ref[rows, at : at + 128] = (o[:, :128] / o[:, 128:]).astype(BF)

    def group(g):
        at = mult(g * STEP, STEP)
        qkv_product(n_ref.at[g], w_ref, qkv_ref, QKV_UNROLL)
        pipeline(6 * tiles, score, soften, weigh)
        out_product(att_ref, w_ref, e_ref.at[g])
        feats = [patch_sum(normalise(e_ref[g, 128 * t : 128 * t + 128])[0]) for t in range(tiles)]
        feat_ref[pl.ds(at, STEP), :D] = jnp.concatenate(feats, axis=0).astype(BF)

    loop(groups, group)
    sums = dot_tn(hot_ref[...], feat_ref[...])
    for b in range(16):
        block = sums[4 * b : 4 * b + 4].astype(csum_ref.dtype)
        csum_ref[b] = block
        csum_ref[16 + b] = block
    save_w.wait()
    save_wp.wait()


def copies_of(pairs, sems):
    copies = [pltpu.make_async_copy(src, dst, sems.at[i]) for i, (src, dst) in enumerate(pairs)]
    for copy in copies:
        copy.start()
    return copies


def synth_kernel(
    where_ref, mine_ref, theirs_ref, images_ref, w_in, wp_in,
    sum_ref, n_out, r1_out, qkv_out, p_out, xhat2_out, r2_out,
    n_ref, r1_ref, qkv_ref, p_ref, xhat2_ref, r2_ref,
    e_ref, att_ref, x_ref, x32_ref, pixels_ref, posx_ref, w_ref, wp_ref, in_sems, sems,
):
    tiles = SYN // 8
    pairs = [
        (images_ref.at[k, :, SYN_AT:], x_ref.at[32 * k : 32 * k + 32]) for k in range(4)
    ]
    loads = copies_of(pairs + [(wp_in, wp_ref), (w_in, w_ref)], in_sems)
    saves = [
        pltpu.make_async_copy(src, dst, sems.at[i])
        for i, (src, dst) in enumerate(
            (
                (n_ref, n_out), (r1_ref, r1_out), (qkv_ref, qkv_out),
                (p_ref, p_out), (xhat2_ref, xhat2_out), (r2_ref, r2_out),
            )
        )
    ]
    spread_position(where_ref, mine_ref, theirs_ref, posx_ref)
    for copy in loads[:5]:
        copy.wait()
    x32_ref[...] = x_ref[...].astype(F32).reshape(4, 32, 512)
    pixels_ref[...] = jnp.zeros_like(pixels_ref)
    for k in range(4):
        for m in range(6):
            for i in range(5):
                pixels_ref[SLOT * k + i : SLOT * k + i + 1, 512 * m : 512 * m + 512] = x32_ref[
                    k, 6 * i + m : 6 * i + m + 1
                ]
    x32 = pixels_ref[...]
    for t, e in enumerate(embed_rows(x32, wp_ref, tiles)):
        rows = slice(128 * t, 128 * t + 128)
        e = e + posx_ref[...]
        e_ref[rows] = e
        xhat, rstd = normalise(e)
        r1_ref[rows] = jnp.broadcast_to(rstd, (128, 128))
        n_ref[rows] = xhat.astype(BF)
    saves[0].start()
    saves[1].start()
    loads[5].wait()
    qkv_product(n_ref, w_ref, qkv_ref, SYN_QKV_UNROLL)
    saves[2].start()
    low = low_half()
    bias = image_bias()

    def score(u):
        rows, at = pl.ds((u // 6) * 128, 128), (u % 6) * 128
        kbd = by_head(qkv_ref[rows, D + at : D + at + 128], low)
        return dot_nt(qkv_ref[rows, at : at + 128], kbd)

    def soften(u, s):
        rows, at = pl.ds((u // 6) * 128, 128), (u % 6) * 256
        parts = [ex / jnp.sum(ex, axis=-1, keepdims=True) for ex in exp_scores(s, bias)]
        p_ref[rows, at : at + 256] = jnp.concatenate(parts, axis=1).astype(BF)

    def weigh(u):
        rows, at = pl.ds((u // 6) * 128, 128), (u % 6) * 128
        vbd = by_head(qkv_ref[rows, 2 * D + at : 2 * D + at + 128], low)
        att_ref[rows, at : at + 128] = dot(p_ref[rows, 2 * at : 2 * at + 256], vbd).astype(BF)

    pipeline(6 * tiles, score, soften, weigh)
    saves[3].start()
    out_product(att_ref, w_ref, e_ref)
    feats = []
    for t in range(tiles):
        rows = slice(128 * t, 128 * t + 128)
        xhat, rstd = normalise(e_ref[rows])
        xhat2_ref[rows] = xhat.astype(BF)
        r2_ref[rows] = jnp.broadcast_to(rstd, (128, 128))
        feats.append(patch_sum(xhat))
    saves[4].start()
    saves[5].start()
    feats = jnp.concatenate(feats, axis=0)
    for s in range(4):
        sum_ref[s : s + 1] = jnp.sum(feats[SLOT * s : SLOT * s + 5], axis=0, keepdims=True)
    for copy in saves:
        copy.wait()


def norm_back(g, xhat, rstd):
    mean_g = jnp.mean(g, axis=-1, keepdims=True)
    mean_gx = jnp.mean(g * xhat, axis=-1, keepdims=True)
    return rstd[:, :1] * (g - mean_g - xhat * mean_gx)


def back_kernel(
    where_ref, means_ref, own_ref, their_ref, w_in, wp_in, n_in, r1_in, qkv_in, p_in, xhat2_in, r2_in,
    out0, out1, out2, out3,
    w_ref, wp_ref, n_ref, r1_ref, qkv_ref, p_ref, xhat2_ref, r2_ref,
    dh_ref, dhb_ref, da_ref, dqkv_ref, dn_ref, spread_ref, px_ref, grad_ref, sems,
):
    tiles = SYN // 8
    out_cols = pl.ds(OUT_AT, D)
    loads = copies_of(
        (
            (xhat2_in, xhat2_ref), (r2_in, r2_ref),
            (w_in.at[:, out_cols], w_ref.at[:, out_cols]),
            (qkv_in, qkv_ref), (p_in, p_ref),
            (w_in.at[:, :OUT_AT], w_ref.at[:, :OUT_AT]),
            (n_in, n_ref), (r1_in, r1_ref), (wp_in, wp_ref),
        ),
        sems,
    )
    image = lax.broadcasted_iota(jnp.int32, (SYN, D), 0)
    spread = jnp.zeros((SYN, D), F32)
    for s in range(4):
        mine = (image >= SLOT * s) & (image < SLOT * s + 5)
        syn = (own_ref[s : s + 1] + their_ref[s : s + 1]) * (1.0 / IPC)
        g = (syn - means_ref[s : s + 1]) * (2.0 / (IPC * TOKENS))
        spread = jnp.where(mine, g, spread)
    spread_ref[...] = spread
    loads[0].wait()
    loads[1].wait()

    def second_norm(t):
        rows = pl.ds(mult(128 * t, 128), 128)
        g = spread_ref[pl.ds(mult(8 * t, 8), 8)]
        g = jnp.broadcast_to(g[None], (TOKENS, 8, D)).reshape(128, D)
        dh = norm_back(g, xhat2_ref[rows].astype(F32), r2_ref[rows])
        dh_ref[rows] = dh
        dhb_ref[rows] = dh.astype(BF)

    loop(tiles, second_norm, tiles)
    loads[2].wait()

    def out_back(c):
        at = mult(256 * c, 128)
        da_ref[:, pl.ds(at, 256)] = dot_nt(
            dhb_ref[...], w_ref[pl.ds(at, 256), OUT_AT : OUT_AT + D]
        ).astype(BF)

    loop(3, out_back, 3)
    loads[3].wait()
    loads[4].wait()
    low = low_half()

    def probs_back(u):
        rows, at = pl.ds((u // 6) * 128, 128), (u % 6) * 128
        da = da_ref[rows, at : at + 128]
        return dot_nt(da, by_head(qkv_ref[rows, 2 * D + at : 2 * D + at + 128], low))

    def scores_back(u, dp):
        rows, at = pl.ds((u // 6) * 128, 128), (u % 6) * 128
        da = da_ref[rows, at : at + 128]
        probs = p_ref[rows, 2 * at : 2 * at + 256]
        dv = dot_tn(probs, da)
        dqkv_ref[rows, 2 * D + at : 2 * D + at + 128] = jnp.where(low, dv[:128], dv[128:]).astype(BF)
        p32 = probs.astype(F32)
        ds = []
        for h in range(2):
            ph, dph = p32[:, 128 * h : 128 * h + 128], dp[:, 128 * h : 128 * h + 128]
            inner = jnp.sum(ph * dph, axis=-1, keepdims=True)
            ds.append(ph * (dph - inner))
        return jnp.concatenate(ds, axis=1).astype(BF)

    def query_key_back(u, ds):
        rows, at = pl.ds((u // 6) * 128, 128), (u % 6) * 128
        kbd = by_head(qkv_ref[rows, D + at : D + at + 128], low)
        dqkv_ref[rows, at : at + 128] = (dot(ds, kbd) * 0.125).astype(BF)
        dk = dot_tn(ds, qkv_ref[rows, at : at + 128])
        dqkv_ref[rows, D + at : D + at + 128] = jnp.where(low, dk[:128], dk[128:]).astype(BF)

    pipeline(6 * tiles, probs_back, scores_back, query_key_back)
    loads[5].wait()

    def qkv_back(c):
        at = mult(256 * c, 128)
        rows = pl.ds(at, 256)
        dn = dot_nt(dqkv_ref[:, : 2 * D], w_ref[rows, : 2 * D])
        dn_ref[:, rows] = dn + dot_nt(dqkv_ref[:, 2 * D :], w_ref[rows, COLS : COLS + D])

    loop(3, qkv_back, 3)
    for copy in loads[6:]:
        copy.wait()

    def first_norm(t):
        rows = pl.ds(mult(128 * t, 128), 128)
        de = dh_ref[rows] + norm_back(dn_ref[rows], n_ref[rows].astype(F32), r1_ref[rows])
        de = de.astype(BF)
        even = dot_nt(de[:64], wp_ref[0])
        odd = dot_nt(de[64:], wp_ref[1])
        px_ref[t] = jnp.concatenate(
            [even[:, :128], even[:, 128:] + odd[:, :128], odd[:, 128:]], axis=1
        )

    loop(tiles, first_norm, tiles)
    for j in range(8):
        cols = slice(384 * j, 384 * j + 384)
        all_rows = jnp.concatenate([px_ref[t, 8 * j : 8 * j + 8] for t in range(tiles)], axis=0)
        for s in range(4):
            grad_ref[8 * s : 8 * s + SLOT, cols] = all_rows[SLOT * s : SLOT * s + SLOT]
    for at, out in zip(ring_order(where_ref[3]), (out0, out1, out2, out3)):
        out[...] = grad_ref[pl.ds(mult(8 * at, 8), 8)][:5].astype(BF)


SMEM_SPEC = pl.BlockSpec(memory_space=pltpu.SMEM)
VMEM_SPEC = pl.BlockSpec(memory_space=pltpu.VMEM)
ANY_SPEC = pl.BlockSpec(memory_space=pltpu.HBM)


def buffer(shape, kind):
    return pltpu.VMEM(shape, kind)


def run_real(place, mine_pos, their_pos, images, mine, theirs):
    rows = STEP * TOKENS
    return pl.pallas_call(
        real_kernel,
        in_specs=[SMEM_SPEC, VMEM_SPEC, VMEM_SPEC] + [ANY_SPEC] * 9,
        out_specs=[pl.BlockSpec((32, 4, D + 128), lambda: (0, 0, 0)), ANY_SPEC, ANY_SPEC],
        out_shape=[
            jax.ShapeDtypeStruct((32, 4, D + 128), BF),
            jax.ShapeDtypeStruct((D, 2 * COLS), BF),
            jax.ShapeDtypeStruct((2, 256, D), BF),
        ],
        scratch_shapes=[
            buffer((REAL // STEP, rows, D), F32),
            buffer((REAL // STEP, rows, D), BF),
            buffer((rows, 3 * D), BF),
            buffer((rows, D), BF),
            buffer((REAL, D + 128), BF),
            buffer((REAL, 128), BF),
            buffer((REAL, PIXELS + 128), BF),
            buffer((128, D), F32),
            buffer((D, 2 * COLS), BF),
            buffer((2, 256, D), BF),
            pltpu.SemaphoreType.DMA((5,)),
        ],
        compiler_params=pltpu.CompilerParams(vmem_limit_bytes=VMEM_LIMIT),
        cost_estimate=pl.CostEstimate(
            flops=14_000_000_000, bytes_accessed=12_000_000, transcendentals=3_000_000
        ),
        name="real_forward",
    )(place, mine_pos, their_pos, images, *mine, *theirs)


SYN_ROWS = SYN * TOKENS
SAVED = [
    ((SYN_ROWS, D), BF),
    ((SYN_ROWS, 128), F32),
    ((SYN_ROWS, 3 * D), BF),
    ((SYN_ROWS, 2 * D), BF),
    ((SYN_ROWS, D), BF),
    ((SYN_ROWS, 128), F32),
]
WEIGHTS = [((D, 2 * COLS), BF), ((2, 256, D), BF)]


def run_synth(place, mine_pos, their_pos, images, w, wp):
    return pl.pallas_call(
        synth_kernel,
        in_specs=[SMEM_SPEC, VMEM_SPEC, VMEM_SPEC] + [ANY_SPEC] * 3,
        out_specs=[pl.BlockSpec((4, D), lambda: (0, 0))] + [ANY_SPEC] * 6,
        out_shape=[jax.ShapeDtypeStruct((4, D), F32)]
        + [jax.ShapeDtypeStruct(s, t) for s, t in SAVED],
        scratch_shapes=[buffer(s, t) for s, t in SAVED]
        + [
            buffer((SYN_ROWS, D), F32),
            buffer((SYN_ROWS, D), BF),
            buffer((128, 512), BF),
            buffer((4, 32, 512), F32),
            buffer((SYN, PIXELS), F32),
            buffer((128, D), F32),
        ]
        + [buffer(s, t) for s, t in WEIGHTS]
        + [pltpu.SemaphoreType.DMA((6,)), pltpu.SemaphoreType.DMA((6,))],
        compiler_params=pltpu.CompilerParams(vmem_limit_bytes=VMEM_LIMIT),
        cost_estimate=pl.CostEstimate(
            flops=3_000_000_000, bytes_accessed=12_000_000, transcendentals=600_000
        ),
        name="synth_forward",
    )(place, mine_pos, their_pos, images, w, wp)


def run_back(place, means, own, their, w, wp, saved):
    return pl.pallas_call(
        back_kernel,
        in_specs=[SMEM_SPEC] + [VMEM_SPEC] * 3 + [ANY_SPEC] * 8,
        out_specs=[pl.BlockSpec((5, PIXELS), lambda: (0, 0))] * 4,
        out_shape=[jax.ShapeDtypeStruct((5, PIXELS), BF)] * 4,
        scratch_shapes=[buffer(s, t) for s, t in WEIGHTS + SAVED]
        + [
            buffer((SYN_ROWS, D), F32),
            buffer((SYN_ROWS, D), BF),
            buffer((SYN_ROWS, D), BF),
            buffer((SYN_ROWS, 3 * D), BF),
            buffer((SYN_ROWS, D), F32),
            buffer((SYN, D), F32),
            buffer((SYN // 8, 64, 384), F32),
            buffer((32, PIXELS), F32),
            pltpu.SemaphoreType.DMA((9,)),
        ],
        compiler_params=pltpu.CompilerParams(vmem_limit_bytes=VMEM_LIMIT),
        cost_estimate=pl.CostEstimate(
            flops=4_000_000_000, bytes_accessed=12_000_000, transcendentals=0
        ),
        name="synth_backward",
    )(place, means, own, their, w, wp, *saved)


def gather_weights(core, x, patch_weight, qkv_weight, out_weight, images):
    columns = jnp.concatenate([qkv_weight, out_weight], axis=-1)
    patch = jnp.pad(patch_weight.reshape(2, 3, 2, 3, 128), ((0, 0),) * 3 + ((0, 1), (0, 0)))
    patch = patch.transpose(0, 1, 3, 2, 4).reshape(2, 12, 2, 128)
    both = jnp.concatenate([columns.reshape(2, 12, 2, 2 * D), patch], axis=-1)
    both = both.transpose(0, 2, 1, 3).reshape(4, 12, COLS)
    parts = []
    for k in range(4):
        to = (x - k) % 4
        first = to // 2 == core
        index = (to % 2) * 2 + jnp.where(first, 0, 1)

        def target(c, yy, zz, xx, k=k):
            to = (xx - k) % 4
            return (0, yy, zz, to) if to // 2 == c else (1, yy, zz, (to + 2) % 4)

        parts.append(permute(lax.dynamic_index_in_dim(both, index, 0, keepdims=False), target))
    ring = jnp.roll(jnp.stack(parts), x + 2 * core, axis=0).reshape(BLOCK_ROWS, COLS)
    near, far = (
        jnp.stack([ring, from_first(ring, 1)]),
        jnp.stack([from_first(ring, 2), from_first(ring, 3)]),
    )
    near = jnp.stack([near, other_second(near)])
    far = jnp.stack([far, across_second(far)])
    near_across, far_other = across_second(near), other_second(far)
    near_across, images, their_pos = lax.optimization_barrier((near_across, *images))
    mine = [near, near_across, far, far_other]
    theirs = [swap_cores(a) for a in mine]
    return mine, theirs, images, their_pos


def local(
    real_images, real_labels, class_ids, synthetic, patch_weight, position, qkv_weight, out_weight
):
    core, img = lax.axis_index("enc"), lax.axis_index("img")
    y, z, x = img // 16, (img // 4) % 4, img % 4
    place = jnp.stack([core, y, z, x]).astype(jnp.int32)

    hit = real_labels[:, None] == class_ids[None, :]
    index = jnp.sum(jnp.where(hit, jnp.arange(64, dtype=F32)[None, :], 0.0), axis=1)
    tagged = jnp.concatenate(
        [real_images, jnp.broadcast_to(index[:, None], (64, 128)).astype(BF)], axis=1
    )
    syn = lax.dynamic_slice_in_dim(synthetic, 5 * core, 5, 0).astype(BF).reshape(30, 512)
    images = jnp.concatenate(
        [lax.dynamic_slice_in_dim(tagged, 32 * core, 32, 0), jnp.pad(syn, ((0, 2), (0, 0)))],
        axis=1,
    )
    rings = [[flat(c, yz // 4, yz % 4, xx) for xx in range(4)] for c in range(2) for yz in range(16)]
    images = lax.all_to_all(
        jnp.broadcast_to(images[None], (4, 32, SYN_AT + 512)), AXES, 0, 0, axis_index_groups=rings
    )
    images = (images, swap_cores(position))
    mine, theirs, images, their_pos = gather_weights(
        core, x, patch_weight, qkv_weight, out_weight, images
    )
    csum, w, wp = run_real(place, position, their_pos, images, mine, theirs)

    groups = [[c * 64 + yz * 4 + xx for c in range(2) for yz in range(16)] for xx in range(4)]
    got = lax.all_to_all(csum, AXES, 0, 0, axis_index_groups=groups)
    total = jnp.sum(got.astype(F32), axis=0)
    means = total[:, :D] / jnp.maximum(total[:, D : D + 1], 1.0)

    own, *saved = run_synth(place, position, their_pos, images, w, wp)
    grads = run_back(place, means, own, swap_cores(own), w, wp, saved)

    beside, means = lax.optimization_barrier((other_x(grads[1]), means))
    sent = []
    for m in range(2):
        row = lax.dynamic_index_in_dim(means, (x - m) % 2 + 2 * core, 0, keepdims=True)
        sent.append(
            permute(row, lambda c, yy, zz, xx, m=m: (xx // 2, yy, zz, (xx - m) % 2 + 2 * c))
        )
    first = jnp.where(x % 2 == 0, sent[0], sent[1])
    second = jnp.where(x % 2 == 0, sent[1], sent[0])
    real_means = jnp.stack([first, second])

    pixel = grads[0].astype(F32) + beside.astype(F32)
    pixel = pixel + across_x(grads[2]).astype(F32) + from_x(grads[3], 2).astype(F32)
    other = swap_cores(pixel)
    pixel_grad = jnp.concatenate(
        [jnp.where(core == 0, pixel, other), jnp.where(core == 0, other, pixel)], axis=0
    )
    return (real_means, pixel_grad)


def solution(mesh):
    return jax.shard_map(
        local,
        mesh=mesh,
        in_specs=(
            P("img", None),
            P("img"),
            P(),
            P("img", None),
            P("enc", "img", None),
            P("enc", None, None),
            P("enc", "img", None),
            P("enc", "img", None),
        ),
        out_specs=(P("enc", "img", None), P("img", None)),
        check_vma=False,
    )
```

```python
import jax
import jax.numpy as jnp
from jax import lax
from jax.experimental import pallas as pl
from jax.experimental.pallas import tpu as pltpu
from jax.sharding import PartitionSpec as P

AXES = ("enc", "img")
BF = jnp.bfloat16
F32 = jnp.float32
D = 768
PIXELS = 3072
IPC = 10
SYN_AT = PIXELS
SLOT = 6
SYN = 4 * SLOT
BLOCK_ROWS = 48
COLS = 2 * D + 128
OUT_AT = COLS + D
STEP = 64
QKV_UNROLL = 9
SYN_QKV_UNROLL = 9
REAL = 128
TOKENS = 16
VMEM_LIMIT = 60 * 1024 * 1024


def flat(c, y, z, x):
    return (c % 2) * 64 + (y % 4) * 16 + (z % 4) * 4 + (x % 4)


PLACES = [(c, y, z, x) for c in range(2) for y in range(4) for z in range(4) for x in range(4)]


def permute(a, target):
    return lax.ppermute(a, AXES, [(flat(*p), flat(*target(*p))) for p in PLACES])


def swap_cores(a):
    return permute(a, lambda c, y, z, x: (1 - c, y, z, x))


def from_x(a, k):
    return permute(a, lambda c, y, z, x: (c, y, z, x - k))


def other_x(a):
    return permute(a, lambda c, y, z, x: (c, y, z, x ^ 1))


def across_x(a):
    return permute(a, lambda c, y, z, x: (c, y, z, 3 - x))


def other_second(a):
    return permute(a, lambda c, y, z, x: (c, y, z ^ 1, x) if c == 0 else (c, y ^ 1, z, x))


def across_second(a):
    return permute(a, lambda c, y, z, x: (c, y, 3 - z, x) if c == 0 else (c, 3 - y, z, x))


def ring_order(at):
    other = at + 1 - 2 * (at % 2)
    return (at, other, 3 - at, 3 - other)


def from_first(a, k):
    return permute(a, lambda c, y, z, x: (c, y - k, z, x) if c == 0 else (c, y, z - k, x))


def from_second(a, k):
    return permute(a, lambda c, y, z, x: (c, y, z - k, x) if c == 0 else (c, y - k, z, x))


def normalise(h):
    mean = jnp.mean(h, axis=-1, keepdims=True)
    centred = h - mean
    var = jnp.mean(centred * centred, axis=-1, keepdims=True)
    rstd = lax.rsqrt(var + 1e-06)
    return centred * rstd, rstd


def dot(a, b):
    return jnp.dot(a, b, preferred_element_type=F32)


def dot_nt(a, b):
    return lax.dot_general(a, b, (((1,), (1,)), ((), ())), preferred_element_type=F32)


def dot_tn(a, b):
    return lax.dot_general(a, b, (((0,), (0,)), ((), ())), preferred_element_type=F32)


def low_half():
    return lax.broadcasted_iota(jnp.int32, (128, 128), 1) < 64


def by_head(a, low):
    zero = jnp.zeros_like(a)
    return jnp.concatenate([jnp.where(low, a, zero), jnp.where(low, zero, a)], axis=0)


def image_bias():
    row = lax.broadcasted_iota(jnp.int32, (128, 128), 0)
    col = lax.broadcasted_iota(jnp.int32, (128, 128), 1)
    return jnp.where(row % 8 == col % 8, 0.0, -1e30).astype(F32)


def embed_rows(x32, wp_ref, tiles):
    halves = []
    for odd in range(2):
        rows = [
            x32[8 * t : 8 * t + 8, 384 * j + 128 * odd : 384 * j + 128 * odd + 256]
            for t in range(tiles)
            for j in range(8)
        ]
        halves.append(dot(jnp.concatenate(rows, axis=0).astype(BF), wp_ref[odd]))
    return [
        jnp.concatenate([h[64 * t : 64 * t + 64] for h in halves], axis=0) for t in range(tiles)
    ]


def exp_scores(s, bias):
    parts = []
    for h in range(2):
        sh = s[:, 128 * h : 128 * h + 128] + bias
        parts.append(jnp.exp(sh - jnp.max(sh, axis=-1, keepdims=True)))
    return parts


def pipeline(count, first, second, third):
    made = {}
    for k in range(count + 2):
        if k < count:
            made[k] = first(k)
        if 0 <= k - 2 < count:
            third(k - 2, *made.pop(k - 2))
        if 0 <= k - 1 < count:
            out = second(k - 1, made.pop(k - 1))
            made[k - 1] = () if out is None else (out,)


def loop(count, fn, unroll=1):
    def body(i, carry):
        fn(i)
        return carry

    lax.fori_loop(0, count, body, 0, unroll=unroll)


def mult(value, of):
    return value if isinstance(value, int) else pl.multiple_of(value, of)


def patch_sum(xhat):
    return jnp.sum(xhat.reshape(TOKENS, 8, D), axis=0) * (1.0 / TOKENS)


def qkv_product(n_ref, w_ref, qkv_ref, unroll):
    def chunk(c):
        at = mult(256 * c, 128)
        col = mult(256 * c + jnp.where(c >= 6, 128, 0), 128)
        out = dot(n_ref[...], w_ref[:, pl.ds(col, 256)])
        qkv_ref[:, pl.ds(at, 256)] = (out * jnp.where(c < 3, 0.125, 1.0)).astype(BF)

    loop(9, chunk, unroll)


def out_product(att_ref, w_ref, e_ref):
    def chunk(c):
        at = mult(256 * c, 128)
        e_ref[:, pl.ds(at, 256)] += dot(att_ref[...], w_ref[:, pl.ds(OUT_AT + at, 256)])

    loop(3, chunk, 3)


def spread_position(where_ref, mine_ref, theirs_ref, posx_ref):
    core, x = where_ref[0], where_ref[3]
    local = x // 2 == core
    pos = jnp.where(local, mine_ref[lax.rem(x, 2)], theirs_ref[lax.rem(x, 2)]).astype(F32)
    for patch in range(TOKENS):
        at = (patch % 2) * 64 + (patch // 2) * 8
        posx_ref[at : at + 8] = jnp.broadcast_to(pos[patch : patch + 1], (8, D))


def real_kernel(
    where_ref, mine_ref, theirs_ref, images_ref, l0, l1, l2, l3, o0, o1, o2, o3,
    csum_ref, w_out, wp_out,
    e_ref, n_ref, qkv_ref, att_ref, feat_ref, tag_ref, x_ref, posx_ref, w_ref, wp_ref, sems,
):
    tiles = STEP // 8
    groups = REAL // STEP
    core, y, z = where_ref[0], where_ref[1], where_ref[2]

    for k in range(4):
        pltpu.make_async_copy(
            images_ref.at[k, :, :SYN_AT], x_ref.at[32 * k : 32 * k + 32], sems.at[1]
        ).start()
        pltpu.make_async_copy(
            images_ref.at[k, 16:32, SYN_AT : SYN_AT + 128],
            tag_ref.at[16 * k : 16 * k + 16],
            sems.at[5],
        ).start()
    near_block = ((0, 0), (0, 1), (1, 0), (1, 1))
    far_block = ((2, 0), (3, 0), (2, 1), (3, 1))
    for cols, sem in ((pl.ds(2 * D, 128), 0), (pl.ds(0, 2 * D), 4)):
        for other, refs in enumerate(((l0, l1, l2, l3), (o0, o1, o2, o3))):
            part = lax.rem(core + other, 2)
            first, second = jnp.where(part == 0, y, z), jnp.where(part == 0, z, y)
            target = pl.ds(pl.multiple_of(part * COLS + cols.start, 128), cols.size)
            for j, at in enumerate(ring_order(second)):
                for i in range(4):
                    line = lax.rem(first + i, 4)
                    block = jnp.where(part == 0, line * 4 + at, at * 4 + line)
                    row = pl.multiple_of(block * BLOCK_ROWS, 16)
                    ref, index = (near_block if i < 2 else far_block)[j]
                    pltpu.make_async_copy(
                        refs[ref].at[index, i % 2, :, cols],
                        w_ref.at[pl.ds(row, BLOCK_ROWS), target],
                        sems.at[sem],
                    ).start()
    wp_ref[...] = jnp.zeros_like(wp_ref)
    spread_position(where_ref, mine_ref, theirs_ref, posx_ref)
    cls = lax.broadcasted_iota(jnp.int32, (128, REAL), 0).astype(F32)
    pltpu.make_async_copy(x_ref, x_ref, sems.at[1]).wait()
    pltpu.make_async_copy(tag_ref, tag_ref, sems.at[5]).wait()
    tags = tag_ref[...].astype(F32)
    index = tags[14:15] + tags[30:31] + tags[46:47] + tags[62:63]
    hot = jnp.where(cls == index, 1.0, 0.0).astype(BF)
    feat_ref[:, D:] = jnp.ones((REAL, 128), BF)
    patch_cols = w_ref.at[:, : 2 * 128]
    pltpu.make_async_copy(patch_cols, patch_cols, sems.at[0]).wait()
    out_row = lax.broadcasted_iota(jnp.int32, (192, D), 0)
    in_row = lax.broadcasted_iota(jnp.int32, (192, D), 1)

    def decode(j):
        pick = jnp.where(in_row == 4 * out_row + j, 1.0, 0.0).astype(BF)
        for part in range(2):
            piece = dot(pick, w_ref[:, part * COLS + 2 * D : (part + 1) * COLS]).astype(BF)
            at = mult(384 * part + 128 * j, 128)
            wp_ref[0, 0:192, pl.ds(at, 128)] = piece
            wp_ref[1, 64:256, pl.ds(at, 128)] = piece

    loop(3, decode, 3)
    save_wp = pltpu.make_async_copy(wp_ref, wp_out, sems.at[3])
    save_wp.start()

    def embed(g):
        at = mult(g * STEP, STEP)
        x32 = x_ref[pl.ds(at, STEP), :PIXELS].astype(F32)
        for t, e in enumerate(embed_rows(x32, wp_ref, tiles)):
            e = e + posx_ref[...]
            e_ref[g, 128 * t : 128 * t + 128] = e
            n_ref[g, 128 * t : 128 * t + 128] = normalise(e)[0].astype(BF)

    loop(groups, embed)
    main_cols = w_ref.at[:, : 4 * D]
    pltpu.make_async_copy(main_cols, main_cols, sems.at[4]).wait()
    save_w = pltpu.make_async_copy(w_ref, w_out, sems.at[2])
    save_w.start()
    low = low_half()
    bias = image_bias()
    ones = by_head(jnp.ones((128, 128), BF), low)

    def score(u):
        rows = pl.ds((u // 6) * 128, 128)
        at = (u % 6) * 128
        kbd = by_head(qkv_ref[rows, D + at : D + at + 128], low)
        return dot_nt(qkv_ref[rows, at : at + 128], kbd)

    def soften(u, s):
        return jnp.concatenate(exp_scores(s, bias), axis=1).astype(BF)

    def weigh(u, ex):
        rows = pl.ds((u // 6) * 128, 128)
        at = (u % 6) * 128
        vbd = by_head(qkv_ref[rows, 2 * D + at : 2 * D + at + 128], low)
        o = dot(ex, jnp.concatenate([vbd, ones], axis=1))
        att_ref[rows, at : at + 128] = (o[:, :128] / o[:, 128:]).astype(BF)

    def group(g):
        at = mult(g * STEP, STEP)
        qkv_product(n_ref.at[g], w_ref, qkv_ref, QKV_UNROLL)
        pipeline(6 * tiles, score, soften, weigh)
        out_product(att_ref, w_ref, e_ref.at[g])
        feats = [patch_sum(normalise(e_ref[g, 128 * t : 128 * t + 128])[0]) for t in range(tiles)]
        feat_ref[pl.ds(at, STEP), :D] = jnp.concatenate(feats, axis=0).astype(BF)

    loop(groups, group)
    sums = dot(hot, feat_ref[...])
    for b in range(16):
        block = sums[4 * b : 4 * b + 4].astype(csum_ref.dtype)
        csum_ref[b] = block
        csum_ref[16 + b] = block
    save_w.wait()
    save_wp.wait()


def copies_of(pairs, sems):
    copies = [pltpu.make_async_copy(src, dst, sems.at[i]) for i, (src, dst) in enumerate(pairs)]
    for copy in copies:
        copy.start()
    return copies


def synth_kernel(
    where_ref, mine_ref, theirs_ref, images_ref, w_in, wp_in,
    sum_ref, n_out, r1_out, qkv_out, p_out, xhat2_out, r2_out,
    n_ref, r1_ref, qkv_ref, p_ref, xhat2_ref, r2_ref,
    e_ref, att_ref, x_ref, x32_ref, pixels_ref, posx_ref, w_ref, wp_ref, in_sems, sems,
):
    tiles = SYN // 8
    pairs = [
        (images_ref.at[k, :, SYN_AT:], x_ref.at[32 * k : 32 * k + 32]) for k in range(4)
    ]
    loads = copies_of(pairs + [(wp_in, wp_ref), (w_in, w_ref)], in_sems)
    saves = [
        pltpu.make_async_copy(src, dst, sems.at[i])
        for i, (src, dst) in enumerate(
            (
                (n_ref, n_out), (r1_ref, r1_out), (qkv_ref, qkv_out),
                (p_ref, p_out), (xhat2_ref, xhat2_out), (r2_ref, r2_out),
            )
        )
    ]
    spread_position(where_ref, mine_ref, theirs_ref, posx_ref)
    for copy in loads[:5]:
        copy.wait()
    x32_ref[...] = x_ref[...].astype(F32).reshape(4, 32, 512)
    pixels_ref[...] = jnp.zeros_like(pixels_ref)
    for k in range(4):
        for m in range(6):
            for i in range(5):
                pixels_ref[SLOT * k + i : SLOT * k + i + 1, 512 * m : 512 * m + 512] = x32_ref[
                    k, 6 * i + m : 6 * i + m + 1
                ]
    x32 = pixels_ref[...]
    for t, e in enumerate(embed_rows(x32, wp_ref, tiles)):
        rows = slice(128 * t, 128 * t + 128)
        e = e + posx_ref[...]
        e_ref[rows] = e
        xhat, rstd = normalise(e)
        r1_ref[rows] = jnp.broadcast_to(rstd, (128, 128))
        n_ref[rows] = xhat.astype(BF)
    saves[0].start()
    saves[1].start()
    loads[5].wait()
    qkv_product(n_ref, w_ref, qkv_ref, SYN_QKV_UNROLL)
    saves[2].start()
    low = low_half()
    bias = image_bias()

    def score(u):
        rows, at = pl.ds((u // 6) * 128, 128), (u % 6) * 128
        kbd = by_head(qkv_ref[rows, D + at : D + at + 128], low)
        return dot_nt(qkv_ref[rows, at : at + 128], kbd)

    def soften(u, s):
        rows, at = pl.ds((u // 6) * 128, 128), (u % 6) * 256
        parts = [ex / jnp.sum(ex, axis=-1, keepdims=True) for ex in exp_scores(s, bias)]
        p_ref[rows, at : at + 256] = jnp.concatenate(parts, axis=1).astype(BF)

    def weigh(u):
        rows, at = pl.ds((u // 6) * 128, 128), (u % 6) * 128
        vbd = by_head(qkv_ref[rows, 2 * D + at : 2 * D + at + 128], low)
        att_ref[rows, at : at + 128] = dot(p_ref[rows, 2 * at : 2 * at + 256], vbd).astype(BF)

    pipeline(6 * tiles, score, soften, weigh)
    saves[3].start()
    out_product(att_ref, w_ref, e_ref)
    feats = []
    for t in range(tiles):
        rows = slice(128 * t, 128 * t + 128)
        xhat, rstd = normalise(e_ref[rows])
        xhat2_ref[rows] = xhat.astype(BF)
        r2_ref[rows] = jnp.broadcast_to(rstd, (128, 128))
        feats.append(patch_sum(xhat))
    saves[4].start()
    saves[5].start()
    feats = jnp.concatenate(feats, axis=0)
    for s in range(4):
        sum_ref[s : s + 1] = jnp.sum(feats[SLOT * s : SLOT * s + 5], axis=0, keepdims=True)
    for copy in saves:
        copy.wait()


def norm_back(g, xhat, rstd):
    mean_g = jnp.mean(g, axis=-1, keepdims=True)
    mean_gx = jnp.mean(g * xhat, axis=-1, keepdims=True)
    return rstd[:, :1] * (g - mean_g - xhat * mean_gx)


def back_kernel(
    where_ref, means_ref, own_ref, their_ref, w_in, wp_in, n_in, r1_in, qkv_in, p_in, xhat2_in, r2_in,
    out0, out1, out2, out3,
    w_ref, wp_ref, n_ref, r1_ref, qkv_ref, p_ref, xhat2_ref, r2_ref,
    dh_ref, dhb_ref, da_ref, dqkv_ref, dn_ref, spread_ref, px_ref, grad_ref, sems,
):
    tiles = SYN // 8
    out_cols = pl.ds(OUT_AT, D)
    loads = copies_of(
        (
            (xhat2_in, xhat2_ref), (r2_in, r2_ref),
            (w_in.at[:, out_cols], w_ref.at[:, out_cols]),
            (qkv_in, qkv_ref), (p_in, p_ref),
            (w_in.at[:, :OUT_AT], w_ref.at[:, :OUT_AT]),
            (n_in, n_ref), (r1_in, r1_ref), (wp_in, wp_ref),
        ),
        sems,
    )
    image = lax.broadcasted_iota(jnp.int32, (SYN, D), 0)
    spread = jnp.zeros((SYN, D), F32)
    for s in range(4):
        mine = (image >= SLOT * s) & (image < SLOT * s + 5)
        syn = (own_ref[s : s + 1] + their_ref[s : s + 1]) * (1.0 / IPC)
        g = (syn - means_ref[s : s + 1]) * (2.0 / (IPC * TOKENS))
        spread = jnp.where(mine, g, spread)
    spread_ref[...] = spread
    loads[0].wait()
    loads[1].wait()

    def second_norm(t):
        rows = pl.ds(mult(128 * t, 128), 128)
        g = spread_ref[pl.ds(mult(8 * t, 8), 8)]
        g = jnp.broadcast_to(g[None], (TOKENS, 8, D)).reshape(128, D)
        dh = norm_back(g, xhat2_ref[rows].astype(F32), r2_ref[rows])
        dh_ref[rows] = dh
        dhb_ref[rows] = dh.astype(BF)

    loop(tiles, second_norm, tiles)
    loads[2].wait()

    def out_back(c):
        at = mult(256 * c, 128)
        da_ref[:, pl.ds(at, 256)] = dot_nt(
            dhb_ref[...], w_ref[pl.ds(at, 256), OUT_AT : OUT_AT + D]
        ).astype(BF)

    loop(3, out_back, 3)
    loads[3].wait()
    loads[4].wait()
    low = low_half()

    def probs_back(u):
        rows, at = pl.ds((u // 6) * 128, 128), (u % 6) * 128
        da = da_ref[rows, at : at + 128]
        return dot_nt(da, by_head(qkv_ref[rows, 2 * D + at : 2 * D + at + 128], low))

    def scores_back(u, dp):
        rows, at = pl.ds((u // 6) * 128, 128), (u % 6) * 128
        da = da_ref[rows, at : at + 128]
        probs = p_ref[rows, 2 * at : 2 * at + 256]
        dv = dot_tn(probs, da)
        dqkv_ref[rows, 2 * D + at : 2 * D + at + 128] = jnp.where(low, dv[:128], dv[128:]).astype(BF)
        p32 = probs.astype(F32)
        ds = []
        for h in range(2):
            ph, dph = p32[:, 128 * h : 128 * h + 128], dp[:, 128 * h : 128 * h + 128]
            inner = jnp.sum(ph * dph, axis=-1, keepdims=True)
            ds.append(ph * (dph - inner))
        return jnp.concatenate(ds, axis=1).astype(BF)

    def query_key_back(u, ds):
        rows, at = pl.ds((u // 6) * 128, 128), (u % 6) * 128
        kbd = by_head(qkv_ref[rows, D + at : D + at + 128], low)
        dqkv_ref[rows, at : at + 128] = (dot(ds, kbd) * 0.125).astype(BF)
        dk = dot_tn(ds, qkv_ref[rows, at : at + 128])
        dqkv_ref[rows, D + at : D + at + 128] = jnp.where(low, dk[:128], dk[128:]).astype(BF)

    pipeline(6 * tiles, probs_back, scores_back, query_key_back)
    loads[5].wait()

    def qkv_back(c):
        at = mult(256 * c, 128)
        rows = pl.ds(at, 256)
        dn = dot_nt(dqkv_ref[:, : 2 * D], w_ref[rows, : 2 * D])
        dn_ref[:, rows] = dn + dot_nt(dqkv_ref[:, 2 * D :], w_ref[rows, COLS : COLS + D])

    loop(3, qkv_back, 3)
    for copy in loads[6:]:
        copy.wait()

    def first_norm(t):
        rows = pl.ds(mult(128 * t, 128), 128)
        de = dh_ref[rows] + norm_back(dn_ref[rows], n_ref[rows].astype(F32), r1_ref[rows])
        de = de.astype(BF)
        even = dot_nt(de[:64], wp_ref[0])
        odd = dot_nt(de[64:], wp_ref[1])
        px_ref[t] = jnp.concatenate(
            [even[:, :128], even[:, 128:] + odd[:, :128], odd[:, 128:]], axis=1
        )

    loop(tiles, first_norm, tiles)
    for j in range(8):
        cols = slice(384 * j, 384 * j + 384)
        all_rows = jnp.concatenate([px_ref[t, 8 * j : 8 * j + 8] for t in range(tiles)], axis=0)
        for s in range(4):
            grad_ref[8 * s : 8 * s + SLOT, cols] = all_rows[SLOT * s : SLOT * s + SLOT]
    for at, out in zip(ring_order(where_ref[3]), (out0, out1, out2, out3)):
        out[...] = grad_ref[pl.ds(mult(8 * at, 8), 8)][:5].astype(BF)


SMEM_SPEC = pl.BlockSpec(memory_space=pltpu.SMEM)
VMEM_SPEC = pl.BlockSpec(memory_space=pltpu.VMEM)
ANY_SPEC = pl.BlockSpec(memory_space=pltpu.HBM)


def buffer(shape, kind):
    return pltpu.VMEM(shape, kind)


def run_real(place, mine_pos, their_pos, images, mine, theirs):
    rows = STEP * TOKENS
    return pl.pallas_call(
        real_kernel,
        in_specs=[SMEM_SPEC, VMEM_SPEC, VMEM_SPEC] + [ANY_SPEC] * 9,
        out_specs=[pl.BlockSpec((32, 4, D + 128), lambda: (0, 0, 0)), ANY_SPEC, ANY_SPEC],
        out_shape=[
            jax.ShapeDtypeStruct((32, 4, D + 128), BF),
            jax.ShapeDtypeStruct((D, 2 * COLS), BF),
            jax.ShapeDtypeStruct((2, 256, D), BF),
        ],
        scratch_shapes=[
            buffer((REAL // STEP, rows, D), F32),
            buffer((REAL // STEP, rows, D), BF),
            buffer((rows, 3 * D), BF),
            buffer((rows, D), BF),
            buffer((REAL, D + 128), BF),
            buffer((64, 128), BF),
            buffer((REAL, PIXELS), BF),
            buffer((128, D), F32),
            buffer((D, 2 * COLS), BF),
            buffer((2, 256, D), BF),
            pltpu.SemaphoreType.DMA((6,)),
        ],
        compiler_params=pltpu.CompilerParams(vmem_limit_bytes=VMEM_LIMIT),
        cost_estimate=pl.CostEstimate(
            flops=14_000_000_000, bytes_accessed=12_000_000, transcendentals=3_000_000
        ),
        name="real_forward",
    )(place, mine_pos, their_pos, images, *mine, *theirs)


SYN_ROWS = SYN * TOKENS
SAVED = [
    ((SYN_ROWS, D), BF),
    ((SYN_ROWS, 128), F32),
    ((SYN_ROWS, 3 * D), BF),
    ((SYN_ROWS, 2 * D), BF),
    ((SYN_ROWS, D), BF),
    ((SYN_ROWS, 128), F32),
]
WEIGHTS = [((D, 2 * COLS), BF), ((2, 256, D), BF)]


def run_synth(place, mine_pos, their_pos, images, w, wp):
    return pl.pallas_call(
        synth_kernel,
        in_specs=[SMEM_SPEC, VMEM_SPEC, VMEM_SPEC] + [ANY_SPEC] * 3,
        out_specs=[pl.BlockSpec((4, D), lambda: (0, 0))] + [ANY_SPEC] * 6,
        out_shape=[jax.ShapeDtypeStruct((4, D), F32)]
        + [jax.ShapeDtypeStruct(s, t) for s, t in SAVED],
        scratch_shapes=[buffer(s, t) for s, t in SAVED]
        + [
            buffer((SYN_ROWS, D), F32),
            buffer((SYN_ROWS, D), BF),
            buffer((128, 512), BF),
            buffer((4, 32, 512), F32),
            buffer((SYN, PIXELS), F32),
            buffer((128, D), F32),
        ]
        + [buffer(s, t) for s, t in WEIGHTS]
        + [pltpu.SemaphoreType.DMA((6,)), pltpu.SemaphoreType.DMA((6,))],
        compiler_params=pltpu.CompilerParams(vmem_limit_bytes=VMEM_LIMIT),
        cost_estimate=pl.CostEstimate(
            flops=3_000_000_000, bytes_accessed=12_000_000, transcendentals=600_000
        ),
        name="synth_forward",
    )(place, mine_pos, their_pos, images, w, wp)


def run_back(place, means, own, their, w, wp, saved):
    return pl.pallas_call(
        back_kernel,
        in_specs=[SMEM_SPEC] + [VMEM_SPEC] * 3 + [ANY_SPEC] * 8,
        out_specs=[pl.BlockSpec((5, PIXELS), lambda: (0, 0))] * 4,
        out_shape=[jax.ShapeDtypeStruct((5, PIXELS), BF)] * 4,
        scratch_shapes=[buffer(s, t) for s, t in WEIGHTS + SAVED]
        + [
            buffer((SYN_ROWS, D), F32),
            buffer((SYN_ROWS, D), BF),
            buffer((SYN_ROWS, D), BF),
            buffer((SYN_ROWS, 3 * D), BF),
            buffer((SYN_ROWS, D), F32),
            buffer((SYN, D), F32),
            buffer((SYN // 8, 64, 384), F32),
            buffer((32, PIXELS), F32),
            pltpu.SemaphoreType.DMA((9,)),
        ],
        compiler_params=pltpu.CompilerParams(vmem_limit_bytes=VMEM_LIMIT),
        cost_estimate=pl.CostEstimate(
            flops=4_000_000_000, bytes_accessed=12_000_000, transcendentals=0
        ),
        name="synth_backward",
    )(place, means, own, their, w, wp, *saved)


def gather_weights(core, x, patch_weight, qkv_weight, out_weight, images):
    columns = jnp.concatenate([qkv_weight, out_weight], axis=-1)
    patch = jnp.pad(patch_weight.reshape(2, 3, 2, 3, 128), ((0, 0),) * 3 + ((0, 1), (0, 0)))
    patch = patch.transpose(0, 1, 3, 2, 4).reshape(2, 12, 2, 128)
    both = jnp.concatenate([columns.reshape(2, 12, 2, 2 * D), patch], axis=-1)
    both = both.transpose(0, 2, 1, 3).reshape(4, 12, COLS)
    parts = []
    for k in range(4):
        to = (x - k) % 4
        first = to // 2 == core
        index = (to % 2) * 2 + jnp.where(first, 0, 1)

        def target(c, yy, zz, xx, k=k):
            to = (xx - k) % 4
            return (0, yy, zz, to) if to // 2 == c else (1, yy, zz, (to + 2) % 4)

        parts.append(permute(lax.dynamic_index_in_dim(both, index, 0, keepdims=False), target))
    ring = jnp.roll(jnp.stack(parts), x + 2 * core, axis=0).reshape(BLOCK_ROWS, COLS)
    near, far = (
        jnp.stack([ring, from_first(ring, 1)]),
        jnp.stack([from_first(ring, 2), from_first(ring, 3)]),
    )
    near = jnp.stack([near, other_second(near)])
    far = jnp.stack([far, across_second(far)])
    near_across, far_other = across_second(near), other_second(far)
    near_across, images, their_pos = lax.optimization_barrier((near_across, *images))
    mine = [near, near_across, far, far_other]
    theirs = [swap_cores(a) for a in mine]
    return mine, theirs, images, their_pos


def local(
    real_images, real_labels, class_ids, synthetic, patch_weight, position, qkv_weight, out_weight
):
    core, img = lax.axis_index("enc"), lax.axis_index("img")
    y, z, x = img // 16, (img // 4) % 4, img % 4
    place = jnp.stack([core, y, z, x]).astype(jnp.int32)

    hit = real_labels[:, None] == class_ids[None, :]
    index = jnp.sum(jnp.where(hit, jnp.arange(64, dtype=F32)[None, :], 0.0), axis=1)
    tag = jnp.tile(lax.dynamic_slice_in_dim(index, 32 * core, 32, 0), 4)
    tag = jnp.pad(jnp.where(jnp.arange(128) // 32 == x, tag, 0.0).astype(BF), (0, 384))
    syn = lax.dynamic_slice_in_dim(synthetic, 5 * core, 5, 0).astype(BF).reshape(30, 512)
    syn = jnp.concatenate([syn, tag[None], jnp.zeros((1, 512), BF)], axis=0)
    images = jnp.concatenate(
        [lax.dynamic_slice_in_dim(real_images, 32 * core, 32, 0), syn], axis=1
    )
    rings = [[flat(c, yz // 4, yz % 4, xx) for xx in range(4)] for c in range(2) for yz in range(16)]
    images = lax.all_to_all(
        jnp.broadcast_to(images[None], (4, 32, SYN_AT + 512)), AXES, 0, 0, axis_index_groups=rings
    )
    images = (images, swap_cores(position))
    mine, theirs, images, their_pos = gather_weights(
        core, x, patch_weight, qkv_weight, out_weight, images
    )
    csum, w, wp = run_real(place, position, their_pos, images, mine, theirs)

    groups = [[c * 64 + yz * 4 + xx for c in range(2) for yz in range(16)] for xx in range(4)]
    got = lax.all_to_all(csum, AXES, 0, 0, axis_index_groups=groups)
    total = jnp.sum(got.astype(F32), axis=0)
    means = total[:, :D] / jnp.maximum(total[:, D : D + 1], 1.0)

    own, *saved = run_synth(place, position, their_pos, images, w, wp)
    grads = run_back(place, means, own, swap_cores(own), w, wp, saved)

    beside, means = lax.optimization_barrier((other_x(grads[1]), means))
    sent = []
    for m in range(2):
        row = lax.dynamic_index_in_dim(means, (x - m) % 2 + 2 * core, 0, keepdims=True)
        sent.append(
            permute(row, lambda c, yy, zz, xx, m=m: (xx // 2, yy, zz, (xx - m) % 2 + 2 * c))
        )
    first = jnp.where(x % 2 == 0, sent[0], sent[1])
    second = jnp.where(x % 2 == 0, sent[1], sent[0])
    real_means = jnp.stack([first, second])

    pixel = grads[0].astype(F32) + beside.astype(F32)
    pixel = pixel + across_x(grads[2]).astype(F32) + from_x(grads[3], 2).astype(F32)
    other = swap_cores(pixel)
    pixel_grad = jnp.concatenate(
        [jnp.where(core == 0, pixel, other), jnp.where(core == 0, other, pixel)], axis=0
    )
    return (real_means, pixel_grad)


def solution(mesh):
    return jax.shard_map(
        local,
        mesh=mesh,
        in_specs=(
            P("img", None),
            P("img"),
            P(),
            P("img", None),
            P("enc", "img", None),
            P("enc", None, None),
            P("enc", "img", None),
            P("enc", "img", None),
        ),
        out_specs=(P("enc", "img", None), P("img", None)),
        check_vma=False,
    )
```

```python
import jax
import jax.numpy as jnp
from jax import lax
from jax.experimental import pallas as pl
from jax.experimental.pallas import tpu as pltpu
from jax.sharding import PartitionSpec as P

AXES = ("enc", "img")
BF = jnp.bfloat16
F32 = jnp.float32
D = 768
PIXELS = 3072
IPC = 10
SYN_AT = PIXELS
SLOT = 6
SYN = 4 * SLOT
BLOCK_ROWS = 48
COLS = 2 * D + 128
OUT_AT = COLS + D
STEP = 64
QKV_UNROLL = 9
SYN_QKV_UNROLL = 9
REAL = 128
TOKENS = 16
VMEM_LIMIT = 60 * 1024 * 1024


def flat(c, y, z, x):
    return (c % 2) * 64 + (y % 4) * 16 + (z % 4) * 4 + (x % 4)


PLACES = [(c, y, z, x) for c in range(2) for y in range(4) for z in range(4) for x in range(4)]


def permute(a, target):
    return lax.ppermute(a, AXES, [(flat(*p), flat(*target(*p))) for p in PLACES])


def swap_cores(a):
    return permute(a, lambda c, y, z, x: (1 - c, y, z, x))


def from_x(a, k):
    return permute(a, lambda c, y, z, x: (c, y, z, x - k))


def other_x(a):
    return permute(a, lambda c, y, z, x: (c, y, z, x ^ 1))


def across_x(a):
    return permute(a, lambda c, y, z, x: (c, y, z, 3 - x))


def other_second(a):
    return permute(a, lambda c, y, z, x: (c, y, z ^ 1, x) if c == 0 else (c, y ^ 1, z, x))


def across_second(a):
    return permute(a, lambda c, y, z, x: (c, y, 3 - z, x) if c == 0 else (c, 3 - y, z, x))


def ring_order(at):
    other = at + 1 - 2 * (at % 2)
    return (at, other, 3 - at, 3 - other)


def from_first(a, k):
    return permute(a, lambda c, y, z, x: (c, y - k, z, x) if c == 0 else (c, y, z - k, x))


def from_second(a, k):
    return permute(a, lambda c, y, z, x: (c, y, z - k, x) if c == 0 else (c, y - k, z, x))


def normalise(h):
    mean = jnp.mean(h, axis=-1, keepdims=True)
    centred = h - mean
    var = jnp.mean(centred * centred, axis=-1, keepdims=True)
    rstd = lax.rsqrt(var + 1e-06)
    return centred * rstd, rstd


def dot(a, b):
    return jnp.dot(a, b, preferred_element_type=F32)


def dot_nt(a, b):
    return lax.dot_general(a, b, (((1,), (1,)), ((), ())), preferred_element_type=F32)


def dot_tn(a, b):
    return lax.dot_general(a, b, (((0,), (0,)), ((), ())), preferred_element_type=F32)


def low_half():
    return lax.broadcasted_iota(jnp.int32, (128, 128), 1) < 64


def by_head(a, low):
    zero = jnp.zeros_like(a)
    return jnp.concatenate([jnp.where(low, a, zero), jnp.where(low, zero, a)], axis=0)


def image_bias():
    row = lax.broadcasted_iota(jnp.int32, (128, 128), 0)
    col = lax.broadcasted_iota(jnp.int32, (128, 128), 1)
    return jnp.where(row % 8 == col % 8, 0.0, -1e30).astype(F32)


def embed_rows(x32, wp_ref, tiles):
    halves = []
    for odd in range(2):
        rows = [
            x32[8 * t : 8 * t + 8, 384 * j + 128 * odd : 384 * j + 128 * odd + 256]
            for t in range(tiles)
            for j in range(8)
        ]
        halves.append(dot(jnp.concatenate(rows, axis=0).astype(BF), wp_ref[odd]))
    return [
        jnp.concatenate([h[64 * t : 64 * t + 64] for h in halves], axis=0) for t in range(tiles)
    ]


def exp_scores(s, bias):
    parts = []
    for h in range(2):
        sh = s[:, 128 * h : 128 * h + 128] + bias
        parts.append(jnp.exp(sh - jnp.max(sh, axis=-1, keepdims=True)))
    return parts


def pipeline(count, first, second, third):
    made = {}
    for k in range(count + 2):
        if k < count:
            made[k] = first(k)
        if 0 <= k - 2 < count:
            third(k - 2, *made.pop(k - 2))
        if 0 <= k - 1 < count:
            out = second(k - 1, made.pop(k - 1))
            made[k - 1] = () if out is None else (out,)


def loop(count, fn, unroll=1):
    def body(i, carry):
        fn(i)
        return carry

    lax.fori_loop(0, count, body, 0, unroll=unroll)


def mult(value, of):
    return value if isinstance(value, int) else pl.multiple_of(value, of)


def patch_sum(xhat):
    return jnp.sum(xhat.reshape(TOKENS, 8, D), axis=0) * (1.0 / TOKENS)


def qkv_product(n_ref, w_ref, qkv_ref, unroll):
    def chunk(c):
        at = mult(256 * c, 128)
        col = mult(256 * c + jnp.where(c >= 6, 128, 0), 128)
        out = dot(n_ref[...], w_ref[:, pl.ds(col, 256)])
        qkv_ref[:, pl.ds(at, 256)] = (out * jnp.where(c < 3, 0.125, 1.0)).astype(BF)

    loop(9, chunk, unroll)


def out_product(att_ref, w_ref, e_ref):
    def chunk(c):
        at = mult(256 * c, 128)
        e_ref[:, pl.ds(at, 256)] += dot(att_ref[...], w_ref[:, pl.ds(OUT_AT + at, 256)])

    loop(3, chunk, 3)


def spread_position(where_ref, mine_ref, theirs_ref, posx_ref):
    core, x = where_ref[0], where_ref[3]
    local = x // 2 == core
    pos = jnp.where(local, mine_ref[lax.rem(x, 2)], theirs_ref[lax.rem(x, 2)]).astype(F32)
    for patch in range(TOKENS):
        at = (patch % 2) * 64 + (patch // 2) * 8
        posx_ref[at : at + 8] = jnp.broadcast_to(pos[patch : patch + 1], (8, D))


def real_kernel(
    where_ref, mine_ref, theirs_ref, images_ref, l0, l1, l2, l3, o0, o1, o2, o3,
    csum_ref, w_out, wp_out,
    e_ref, n_ref, qkv_ref, att_ref, feat_ref, tag_ref, x_ref, posx_ref, w_ref, wp_ref, sems,
):
    tiles = STEP // 8
    groups = REAL // STEP
    core, y, z = where_ref[0], where_ref[1], where_ref[2]

    for k in range(4):
        pltpu.make_async_copy(
            images_ref.at[k, :, :SYN_AT], x_ref.at[32 * k : 32 * k + 32], sems.at[1]
        ).start()
        pltpu.make_async_copy(
            images_ref.at[k, 16:32, SYN_AT : SYN_AT + 128],
            tag_ref.at[16 * k : 16 * k + 16],
            sems.at[5],
        ).start()
    near_block = ((0, 0), (0, 1), (1, 0), (1, 1))
    far_block = ((2, 0), (3, 0), (2, 1), (3, 1))
    for cols, sem in ((pl.ds(2 * D, 128), 0), (pl.ds(0, 2 * D), 4)):
        for other, refs in enumerate(((l0, l1, l2, l3), (o0, o1, o2, o3))):
            part = lax.rem(core + other, 2)
            first, second = jnp.where(part == 0, y, z), jnp.where(part == 0, z, y)
            target = pl.ds(pl.multiple_of(part * COLS + cols.start, 128), cols.size)
            for j, at in enumerate(ring_order(second)):
                for i in range(4):
                    line = lax.rem(first + i, 4)
                    block = jnp.where(part == 0, line * 4 + at, at * 4 + line)
                    row = pl.multiple_of(block * BLOCK_ROWS, 16)
                    ref, index = (near_block if i < 2 else far_block)[j]
                    pltpu.make_async_copy(
                        refs[ref].at[index, i % 2, :, cols],
                        w_ref.at[pl.ds(row, BLOCK_ROWS), target],
                        sems.at[sem],
                    ).start()
    wp_ref[...] = jnp.zeros_like(wp_ref)
    spread_position(where_ref, mine_ref, theirs_ref, posx_ref)
    cls = lax.broadcasted_iota(jnp.int32, (128, REAL), 0).astype(F32)
    pltpu.make_async_copy(x_ref, x_ref, sems.at[1]).wait()
    pltpu.make_async_copy(tag_ref, tag_ref, sems.at[5]).wait()
    tags = tag_ref[...].astype(F32)
    index = tags[14:15] + tags[30:31] + tags[46:47] + tags[62:63]
    hot = jnp.where(cls == index, 1.0, 0.0).astype(BF)
    feat_ref[:, D:] = jnp.ones((REAL, 128), BF)
    patch_cols = w_ref.at[:, : 2 * 128]
    pltpu.make_async_copy(patch_cols, patch_cols, sems.at[0]).wait()
    out_row = lax.broadcasted_iota(jnp.int32, (192, D), 0)
    in_row = lax.broadcasted_iota(jnp.int32, (192, D), 1)

    def decode(j):
        pick = jnp.where(in_row == 4 * out_row + j, 1.0, 0.0).astype(BF)
        for part in range(2):
            piece = dot(pick, w_ref[:, part * COLS + 2 * D : (part + 1) * COLS]).astype(BF)
            at = mult(384 * part + 128 * j, 128)
            wp_ref[0, 0:192, pl.ds(at, 128)] = piece
            wp_ref[1, 64:256, pl.ds(at, 128)] = piece

    loop(3, decode, 3)
    save_wp = pltpu.make_async_copy(wp_ref, wp_out, sems.at[3])
    save_wp.start()

    def embed(g):
        at = mult(g * STEP, STEP)
        x32 = x_ref[pl.ds(at, STEP), :PIXELS].astype(F32)
        for t, e in enumerate(embed_rows(x32, wp_ref, tiles)):
            e = e + posx_ref[...]
            e_ref[g, 128 * t : 128 * t + 128] = e
            n_ref[g, 128 * t : 128 * t + 128] = normalise(e)[0].astype(BF)

    loop(groups, embed)
    main_cols = w_ref.at[:, : 4 * D]
    pltpu.make_async_copy(main_cols, main_cols, sems.at[4]).wait()
    save_w = pltpu.make_async_copy(w_ref, w_out, sems.at[2])
    save_w.start()
    low = low_half()
    bias = image_bias()
    ones = by_head(jnp.ones((128, 128), BF), low)

    def score(u):
        rows = pl.ds((u // 6) * 128, 128)
        at = (u % 6) * 128
        kbd = by_head(qkv_ref[rows, D + at : D + at + 128], low)
        return dot_nt(qkv_ref[rows, at : at + 128], kbd)

    def soften(u, s):
        return jnp.concatenate(exp_scores(s, bias), axis=1).astype(BF)

    def weigh(u, ex):
        rows = pl.ds((u // 6) * 128, 128)
        at = (u % 6) * 128
        vbd = by_head(qkv_ref[rows, 2 * D + at : 2 * D + at + 128], low)
        o = dot(ex, jnp.concatenate([vbd, ones], axis=1))
        att_ref[rows, at : at + 128] = (o[:, :128] * pl.reciprocal(o[:, 128:])).astype(BF)

    def group(g):
        at = mult(g * STEP, STEP)
        qkv_product(n_ref.at[g], w_ref, qkv_ref, QKV_UNROLL)
        pipeline(6 * tiles, score, soften, weigh)
        out_product(att_ref, w_ref, e_ref.at[g])
        feats = [patch_sum(normalise(e_ref[g, 128 * t : 128 * t + 128])[0]) for t in range(tiles)]
        feat_ref[pl.ds(at, STEP), :D] = jnp.concatenate(feats, axis=0).astype(BF)

    loop(groups, group)
    sums = dot(hot, feat_ref[...])
    for b in range(16):
        block = sums[4 * b : 4 * b + 4].astype(csum_ref.dtype)
        csum_ref[b] = block
        csum_ref[16 + b] = block
    save_w.wait()
    save_wp.wait()


def copies_of(pairs, sems):
    copies = [pltpu.make_async_copy(src, dst, sems.at[i]) for i, (src, dst) in enumerate(pairs)]
    for copy in copies:
        copy.start()
    return copies


def synth_kernel(
    where_ref, mine_ref, theirs_ref, images_ref, w_in, wp_in,
    sum_ref, n_out, r1_out, qkv_out, p_out, xhat2_out, r2_out,
    n_ref, r1_ref, qkv_ref, p_ref, xhat2_ref, r2_ref,
    e_ref, att_ref, x_ref, x32_ref, pixels_ref, posx_ref, w_ref, wp_ref, in_sems, sems,
):
    tiles = SYN // 8
    pairs = [
        (images_ref.at[k, :, SYN_AT:], x_ref.at[32 * k : 32 * k + 32]) for k in range(4)
    ]
    loads = copies_of(pairs + [(wp_in, wp_ref), (w_in, w_ref)], in_sems)
    saves = [
        pltpu.make_async_copy(src, dst, sems.at[i])
        for i, (src, dst) in enumerate(
            (
                (n_ref, n_out), (r1_ref, r1_out), (qkv_ref, qkv_out),
                (p_ref, p_out), (xhat2_ref, xhat2_out), (r2_ref, r2_out),
            )
        )
    ]
    spread_position(where_ref, mine_ref, theirs_ref, posx_ref)
    for copy in loads[:5]:
        copy.wait()
    x32_ref[...] = x_ref[...].astype(F32).reshape(4, 32, 512)
    pixels_ref[...] = jnp.zeros_like(pixels_ref)
    for k in range(4):
        for m in range(6):
            for i in range(5):
                pixels_ref[SLOT * k + i : SLOT * k + i + 1, 512 * m : 512 * m + 512] = x32_ref[
                    k, 6 * i + m : 6 * i + m + 1
                ]
    x32 = pixels_ref[...]
    for t, e in enumerate(embed_rows(x32, wp_ref, tiles)):
        rows = slice(128 * t, 128 * t + 128)
        e = e + posx_ref[...]
        e_ref[rows] = e
        xhat, rstd = normalise(e)
        r1_ref[rows] = jnp.broadcast_to(rstd, (128, 128))
        n_ref[rows] = xhat.astype(BF)
    saves[0].start()
    saves[1].start()
    loads[5].wait()
    qkv_product(n_ref, w_ref, qkv_ref, SYN_QKV_UNROLL)
    saves[2].start()
    low = low_half()
    bias = image_bias()

    def score(u):
        rows, at = pl.ds((u // 6) * 128, 128), (u % 6) * 128
        kbd = by_head(qkv_ref[rows, D + at : D + at + 128], low)
        return dot_nt(qkv_ref[rows, at : at + 128], kbd)

    def soften(u, s):
        rows, at = pl.ds((u // 6) * 128, 128), (u % 6) * 256
        parts = [ex / jnp.sum(ex, axis=-1, keepdims=True) for ex in exp_scores(s, bias)]
        p_ref[rows, at : at + 256] = jnp.concatenate(parts, axis=1).astype(BF)

    def weigh(u):
        rows, at = pl.ds((u // 6) * 128, 128), (u % 6) * 128
        vbd = by_head(qkv_ref[rows, 2 * D + at : 2 * D + at + 128], low)
        att_ref[rows, at : at + 128] = dot(p_ref[rows, 2 * at : 2 * at + 256], vbd).astype(BF)

    pipeline(6 * tiles, score, soften, weigh)
    saves[3].start()
    out_product(att_ref, w_ref, e_ref)
    feats = []
    for t in range(tiles):
        rows = slice(128 * t, 128 * t + 128)
        xhat, rstd = normalise(e_ref[rows])
        xhat2_ref[rows] = xhat.astype(BF)
        r2_ref[rows] = jnp.broadcast_to(rstd, (128, 128))
        pltpu.make_async_copy(xhat2_ref.at[rows], xhat2_out.at[rows], sems.at[4]).start()
        pltpu.make_async_copy(r2_ref.at[rows], r2_out.at[rows], sems.at[5]).start()
        feats.append(patch_sum(xhat))
    feats = jnp.concatenate(feats, axis=0)
    for s in range(4):
        sum_ref[s : s + 1] = jnp.sum(feats[SLOT * s : SLOT * s + 5], axis=0, keepdims=True)
    for copy in saves:
        copy.wait()


def norm_back(g, xhat, rstd):
    mean_g = jnp.mean(g, axis=-1, keepdims=True)
    mean_gx = jnp.mean(g * xhat, axis=-1, keepdims=True)
    return rstd[:, :1] * (g - mean_g - xhat * mean_gx)


def back_kernel(
    where_ref, means_ref, own_ref, their_ref, w_in, wp_in, n_in, r1_in, qkv_in, p_in, xhat2_in, r2_in,
    out0, out1, out2, out3,
    w_ref, wp_ref, n_ref, r1_ref, qkv_ref, p_ref, xhat2_ref, r2_ref,
    dh_ref, dhb_ref, da_ref, dqkv_ref, dn_ref, spread_ref, px_ref, grad_ref, sems,
):
    tiles = SYN // 8
    out_cols = pl.ds(OUT_AT, D)
    loads = copies_of(
        (
            (xhat2_in, xhat2_ref), (r2_in, r2_ref),
            (w_in.at[:, out_cols], w_ref.at[:, out_cols]),
            (qkv_in, qkv_ref), (p_in, p_ref),
            (w_in.at[:, :OUT_AT], w_ref.at[:, :OUT_AT]),
            (n_in, n_ref), (r1_in, r1_ref), (wp_in, wp_ref),
        ),
        sems,
    )
    image = lax.broadcasted_iota(jnp.int32, (SYN, D), 0)
    spread = jnp.zeros((SYN, D), F32)
    for s in range(4):
        mine = (image >= SLOT * s) & (image < SLOT * s + 5)
        syn = (own_ref[s : s + 1] + their_ref[s : s + 1]) * (1.0 / IPC)
        g = (syn - means_ref[s : s + 1]) * (2.0 / (IPC * TOKENS))
        spread = jnp.where(mine, g, spread)
    spread_ref[...] = spread
    loads[0].wait()
    loads[1].wait()

    def second_norm(t):
        rows = pl.ds(mult(128 * t, 128), 128)
        g = spread_ref[pl.ds(mult(8 * t, 8), 8)]
        g = jnp.broadcast_to(g[None], (TOKENS, 8, D)).reshape(128, D)
        dh = norm_back(g, xhat2_ref[rows].astype(F32), r2_ref[rows])
        dh_ref[rows] = dh
        dhb_ref[rows] = dh.astype(BF)

    loop(tiles, second_norm, tiles)
    loads[2].wait()

    def out_back(c):
        at = mult(256 * c, 128)
        da_ref[:, pl.ds(at, 256)] = dot_nt(
            dhb_ref[...], w_ref[pl.ds(at, 256), OUT_AT : OUT_AT + D]
        ).astype(BF)

    loop(3, out_back, 3)
    loads[3].wait()
    loads[4].wait()
    low = low_half()

    def probs_back(u):
        rows, at = pl.ds((u // 6) * 128, 128), (u % 6) * 128
        da = da_ref[rows, at : at + 128]
        return dot_nt(da, by_head(qkv_ref[rows, 2 * D + at : 2 * D + at + 128], low))

    def scores_back(u, dp):
        rows, at = pl.ds((u // 6) * 128, 128), (u % 6) * 128
        da = da_ref[rows, at : at + 128]
        probs = p_ref[rows, 2 * at : 2 * at + 256]
        dv = dot_tn(probs, da)
        dqkv_ref[rows, 2 * D + at : 2 * D + at + 128] = jnp.where(low, dv[:128], dv[128:]).astype(BF)
        p32 = probs.astype(F32)
        ds = []
        for h in range(2):
            ph, dph = p32[:, 128 * h : 128 * h + 128], dp[:, 128 * h : 128 * h + 128]
            inner = jnp.sum(ph * dph, axis=-1, keepdims=True)
            ds.append(ph * (dph - inner))
        return jnp.concatenate(ds, axis=1).astype(BF)

    def query_key_back(u, ds):
        rows, at = pl.ds((u // 6) * 128, 128), (u % 6) * 128
        kbd = by_head(qkv_ref[rows, D + at : D + at + 128], low)
        dqkv_ref[rows, at : at + 128] = (dot(ds, kbd) * 0.125).astype(BF)
        dk = dot_tn(ds, qkv_ref[rows, at : at + 128])
        dqkv_ref[rows, D + at : D + at + 128] = jnp.where(low, dk[:128], dk[128:]).astype(BF)

    pipeline(6 * tiles, probs_back, scores_back, query_key_back)
    loads[5].wait()

    def qkv_back(c):
        at = mult(256 * c, 128)
        rows = pl.ds(at, 256)
        dn = dot_nt(dqkv_ref[:, : 2 * D], w_ref[rows, : 2 * D])
        dn_ref[:, rows] = dn + dot_nt(dqkv_ref[:, 2 * D :], w_ref[rows, COLS : COLS + D])

    loop(3, qkv_back, 3)
    for copy in loads[6:]:
        copy.wait()

    def first_norm(t):
        rows = pl.ds(mult(128 * t, 128), 128)
        de = dh_ref[rows] + norm_back(dn_ref[rows], n_ref[rows].astype(F32), r1_ref[rows])
        de = de.astype(BF)
        even = dot_nt(de[:64], wp_ref[0])
        odd = dot_nt(de[64:], wp_ref[1])
        px_ref[t] = jnp.concatenate(
            [even[:, :128], even[:, 128:] + odd[:, :128], odd[:, 128:]], axis=1
        )

    loop(tiles, first_norm, tiles)
    for j in range(8):
        cols = slice(384 * j, 384 * j + 384)
        all_rows = jnp.concatenate([px_ref[t, 8 * j : 8 * j + 8] for t in range(tiles)], axis=0)
        for s in range(4):
            grad_ref[8 * s : 8 * s + SLOT, cols] = all_rows[SLOT * s : SLOT * s + SLOT]
    for at, out in zip(ring_order(where_ref[3]), (out0, out1, out2, out3)):
        out[...] = grad_ref[pl.ds(mult(8 * at, 8), 8)][:5].astype(BF)


SMEM_SPEC = pl.BlockSpec(memory_space=pltpu.SMEM)
VMEM_SPEC = pl.BlockSpec(memory_space=pltpu.VMEM)
ANY_SPEC = pl.BlockSpec(memory_space=pltpu.HBM)


def buffer(shape, kind):
    return pltpu.VMEM(shape, kind)


def run_real(place, mine_pos, their_pos, images, mine, theirs):
    rows = STEP * TOKENS
    return pl.pallas_call(
        real_kernel,
        in_specs=[SMEM_SPEC, VMEM_SPEC, VMEM_SPEC] + [ANY_SPEC] * 9,
        out_specs=[pl.BlockSpec((32, 4, D + 128), lambda: (0, 0, 0)), ANY_SPEC, ANY_SPEC],
        out_shape=[
            jax.ShapeDtypeStruct((32, 4, D + 128), BF),
            jax.ShapeDtypeStruct((D, 2 * COLS), BF),
            jax.ShapeDtypeStruct((2, 256, D), BF),
        ],
        scratch_shapes=[
            buffer((REAL // STEP, rows, D), F32),
            buffer((REAL // STEP, rows, D), BF),
            buffer((rows, 3 * D), BF),
            buffer((rows, D), BF),
            buffer((REAL, D + 128), BF),
            buffer((64, 128), BF),
            buffer((REAL, PIXELS), BF),
            buffer((128, D), F32),
            buffer((D, 2 * COLS), BF),
            buffer((2, 256, D), BF),
            pltpu.SemaphoreType.DMA((6,)),
        ],
        compiler_params=pltpu.CompilerParams(vmem_limit_bytes=VMEM_LIMIT),
        cost_estimate=pl.CostEstimate(
            flops=14_000_000_000, bytes_accessed=12_000_000, transcendentals=3_000_000
        ),
        name="real_forward",
    )(place, mine_pos, their_pos, images, *mine, *theirs)


SYN_ROWS = SYN * TOKENS
SAVED = [
    ((SYN_ROWS, D), BF),
    ((SYN_ROWS, 128), F32),
    ((SYN_ROWS, 3 * D), BF),
    ((SYN_ROWS, 2 * D), BF),
    ((SYN_ROWS, D), BF),
    ((SYN_ROWS, 128), F32),
]
WEIGHTS = [((D, 2 * COLS), BF), ((2, 256, D), BF)]


def run_synth(place, mine_pos, their_pos, images, w, wp):
    return pl.pallas_call(
        synth_kernel,
        in_specs=[SMEM_SPEC, VMEM_SPEC, VMEM_SPEC] + [ANY_SPEC] * 3,
        out_specs=[pl.BlockSpec((4, D), lambda: (0, 0))] + [ANY_SPEC] * 6,
        out_shape=[jax.ShapeDtypeStruct((4, D), F32)]
        + [jax.ShapeDtypeStruct(s, t) for s, t in SAVED],
        scratch_shapes=[buffer(s, t) for s, t in SAVED]
        + [
            buffer((SYN_ROWS, D), F32),
            buffer((SYN_ROWS, D), BF),
            buffer((128, 512), BF),
            buffer((4, 32, 512), F32),
            buffer((SYN, PIXELS), F32),
            buffer((128, D), F32),
        ]
        + [buffer(s, t) for s, t in WEIGHTS]
        + [pltpu.SemaphoreType.DMA((6,)), pltpu.SemaphoreType.DMA((6,))],
        compiler_params=pltpu.CompilerParams(vmem_limit_bytes=VMEM_LIMIT),
        cost_estimate=pl.CostEstimate(
            flops=3_000_000_000, bytes_accessed=12_000_000, transcendentals=600_000
        ),
        name="synth_forward",
    )(place, mine_pos, their_pos, images, w, wp)


def run_back(place, means, own, their, w, wp, saved):
    return pl.pallas_call(
        back_kernel,
        in_specs=[SMEM_SPEC] + [VMEM_SPEC] * 3 + [ANY_SPEC] * 8,
        out_specs=[pl.BlockSpec((5, PIXELS), lambda: (0, 0))] * 4,
        out_shape=[jax.ShapeDtypeStruct((5, PIXELS), BF)] * 4,
        scratch_shapes=[buffer(s, t) for s, t in WEIGHTS + SAVED]
        + [
            buffer((SYN_ROWS, D), F32),
            buffer((SYN_ROWS, D), BF),
            buffer((SYN_ROWS, D), BF),
            buffer((SYN_ROWS, 3 * D), BF),
            buffer((SYN_ROWS, D), F32),
            buffer((SYN, D), F32),
            buffer((SYN // 8, 64, 384), F32),
            buffer((32, PIXELS), F32),
            pltpu.SemaphoreType.DMA((9,)),
        ],
        compiler_params=pltpu.CompilerParams(vmem_limit_bytes=VMEM_LIMIT),
        cost_estimate=pl.CostEstimate(
            flops=4_000_000_000, bytes_accessed=12_000_000, transcendentals=0
        ),
        name="synth_backward",
    )(place, means, own, their, w, wp, *saved)


def gather_weights(core, x, patch_weight, qkv_weight, out_weight, images):
    columns = jnp.concatenate([qkv_weight, out_weight], axis=-1)
    patch = jnp.pad(patch_weight.reshape(2, 3, 2, 3, 128), ((0, 0),) * 3 + ((0, 1), (0, 0)))
    patch = patch.transpose(0, 1, 3, 2, 4).reshape(2, 12, 2, 128)
    both = jnp.concatenate([columns.reshape(2, 12, 2, 2 * D), patch], axis=-1)
    both = both.transpose(0, 2, 1, 3).reshape(4, 12, COLS)
    parts = []
    for k in range(4):
        to = (x - k) % 4
        first = to // 2 == core
        index = (to % 2) * 2 + jnp.where(first, 0, 1)

        def target(c, yy, zz, xx, k=k):
            to = (xx - k) % 4
            return (0, yy, zz, to) if to // 2 == c else (1, yy, zz, (to + 2) % 4)

        parts.append(permute(lax.dynamic_index_in_dim(both, index, 0, keepdims=False), target))
    ring = jnp.roll(jnp.stack(parts), x + 2 * core, axis=0).reshape(BLOCK_ROWS, COLS)
    near, far = (
        jnp.stack([ring, from_first(ring, 1)]),
        jnp.stack([from_first(ring, 2), from_first(ring, 3)]),
    )
    near = jnp.stack([near, other_second(near)])
    far = jnp.stack([far, across_second(far)])
    near_across, far_other = across_second(near), other_second(far)
    near_across, images, their_pos = lax.optimization_barrier((near_across, *images))
    mine = [near, near_across, far, far_other]
    theirs = [swap_cores(a) for a in mine]
    return mine, theirs, images, their_pos


def local(
    real_images, real_labels, class_ids, synthetic, patch_weight, position, qkv_weight, out_weight
):
    core, img = lax.axis_index("enc"), lax.axis_index("img")
    y, z, x = img // 16, (img // 4) % 4, img % 4
    place = jnp.stack([core, y, z, x]).astype(jnp.int32)

    hit = real_labels[:, None] == class_ids[None, :]
    index = jnp.sum(jnp.where(hit, jnp.arange(64, dtype=F32)[None, :], 0.0), axis=1)
    tag = jnp.tile(lax.dynamic_slice_in_dim(index, 32 * core, 32, 0), 4)
    tag = jnp.pad(jnp.where(jnp.arange(128) // 32 == x, tag, 0.0).astype(BF), (0, 384))
    syn = lax.dynamic_slice_in_dim(synthetic, 5 * core, 5, 0).astype(BF).reshape(30, 512)
    syn = jnp.concatenate([syn, tag[None], jnp.zeros((1, 512), BF)], axis=0)
    images = jnp.concatenate(
        [lax.dynamic_slice_in_dim(real_images, 32 * core, 32, 0), syn], axis=1
    )
    rings = [[flat(c, yz // 4, yz % 4, xx) for xx in range(4)] for c in range(2) for yz in range(16)]
    images = lax.all_to_all(
        jnp.broadcast_to(images[None], (4, 32, SYN_AT + 512)), AXES, 0, 0, axis_index_groups=rings
    )
    images = (images, swap_cores(position))
    mine, theirs, images, their_pos = gather_weights(
        core, x, patch_weight, qkv_weight, out_weight, images
    )
    csum, w, wp = run_real(place, position, their_pos, images, mine, theirs)

    groups = [[c * 64 + yz * 4 + xx for c in range(2) for yz in range(16)] for xx in range(4)]
    got = lax.all_to_all(csum, AXES, 0, 0, axis_index_groups=groups)
    total = jnp.sum(got.astype(F32), axis=0)
    means = total[:, :D] / jnp.maximum(total[:, D : D + 1], 1.0)

    own, *saved = run_synth(place, position, their_pos, images, w, wp)
    grads = run_back(place, means, own, swap_cores(own), w, wp, saved)

    beside, means = lax.optimization_barrier((other_x(grads[1]), means))
    sent = []
    for m in range(2):
        row = lax.dynamic_index_in_dim(means, (x - m) % 2 + 2 * core, 0, keepdims=True)
        sent.append(
            permute(row, lambda c, yy, zz, xx, m=m: (xx // 2, yy, zz, (xx - m) % 2 + 2 * c))
        )
    first = jnp.where(x % 2 == 0, sent[0], sent[1])
    second = jnp.where(x % 2 == 0, sent[1], sent[0])
    real_means = jnp.stack([first, second])

    pixel = grads[0].astype(F32) + beside.astype(F32)
    pixel = pixel + across_x(grads[2]).astype(F32) + from_x(grads[3], 2).astype(F32)
    other = swap_cores(pixel)
    pixel_grad = jnp.concatenate(
        [jnp.where(core == 0, pixel, other), jnp.where(core == 0, other, pixel)], axis=0
    )
    return (real_means, pixel_grad)


def solution(mesh):
    return jax.shard_map(
        local,
        mesh=mesh,
        in_specs=(
            P("img", None),
            P("img"),
            P(),
            P("img", None),
            P("enc", "img", None),
            P("enc", None, None),
            P("enc", "img", None),
            P("enc", "img", None),
        ),
        out_specs=(P("enc", "img", None), P("img", None)),
        check_vma=False,
    )
```
